256 devices in a mesh: depth: 64 (over x_hi, y, z), band: 4 (over x_lo, core).
Axes of the slice: x: 4 (x_hi: 2, x_lo: 2; x = x_hi * 2 + x_lo), y: 4, z: 8, core: 2. Of those that a mesh axis runs over, the one named last changes fastest.
Arguments:
- planes: float32 [64, 256, 2048], P('depth', 'band'), may hold values from -6 to 6
- denoised: float32 [64, 256, 2048], P('depth', 'band'), may hold values from -6 to 6
- scaled_dual: float32 [64, 256, 2048], P('depth', 'band'), may hold values from -4 to 4
- measured: float32 [256, 2048], P('band'), may hold values from -6 to 6
- lenslet_psf: bfloat16 [64, 31, 31], P('depth'), may hold values from -0.0234375 to 0.0234375
- kernel: bfloat16 [27, 16], replicated, may hold values from -1.25 to 1.25
- layer_bias: float32 [16], replicated, may hold values from -3 to 3
- mix_weight: bfloat16 [16], replicated, may hold values from -1.5 to 1.5
Outputs:
- new_planes: float32 [64, 256, 2048], P('depth', 'band')
- new_denoised: float32 [64, 256, 2048], P('depth', 'band')
- new_dual: float32 [64, 256, 2048], P('depth', 'band')
The draws below stay inside these ranges and needn't reach their ends.
All inputs are finite; a program needn't handle non-finite values.
Results may differ from the reference program's by a relative error of at most 0.0049.
Values may be sent and summed in bfloat16 or wider, within the bound.
No kernel may reach another device: no remote copies, remote signals or barrier semaphores. Data moves between devices by JAX's collectives and lax.ppermute only.
A program may use at most 128 MiB of HBM per device.

```python
import jax
import jax.numpy as jnp
from jax import lax

COLS = 2048
KS = 31
CH = 16
PLANES = 64
ROWS = 256


def steps_of(stream_key, shape, split, low, largest):
    factor_of = 1.0
    for dim, parts in split:
        draws = jax.random.uniform(jax.random.fold_in(jax.random.fold_in(stream_key, 6), dim), (parts,), jnp.float32, low / len(split), largest / len(split))
        factor_of = factor_of * jnp.repeat(jnp.exp(draws), shape[dim] // parts).reshape((-1,) + (1,) * (len(shape) - 1 - dim))
    return factor_of


def normal_values(stream_key, extent, width, reach, cuts=(), held_as=jnp.bfloat16):
    drawn = width * jax.random.normal(stream_key, extent, jnp.float32)
    if cuts:
        drawn = drawn * steps_of(stream_key, extent, cuts, -0.22, 0.18)
    return jnp.clip(drawn, -reach, reach).astype(held_as)


def setup_inputs(seed: int = 0) -> dict:
    splits = jax.random.split(jax.random.key(seed), 9)
    return {
        "planes": normal_values(splits[0], (PLANES, ROWS, COLS), 1.0, 6.0, ((0, 64), (1, 4)), jnp.float32),
        "denoised": normal_values(splits[1], (PLANES, ROWS, COLS), 1.0, 6.0, ((0, 64), (1, 4)), jnp.float32),
        "scaled_dual": normal_values(splits[2], (PLANES, ROWS, COLS), 0.5, 4.0, ((0, 64), (1, 4)), jnp.float32),
        "measured": normal_values(splits[3], (ROWS, COLS), 1.0, 6.0, ((0, 4),), jnp.float32),
        "lenslet_psf": normal_values(splits[4], (PLANES, KS, KS), (KS * KS * PLANES) ** -0.5, 0.0234375, ((0, 64),)),
        "kernel": normal_values(splits[5], (27, CH), 27 ** -0.5, 1.25),
        "layer_bias": normal_values(splits[6], (CH,), 0.5, 3.0, (), jnp.float32),
        "mix_weight": normal_values(splits[7], (CH,), CH ** -0.5, 1.5),
    }


step_size = 4.0
penalty = 0.5


def reference(planes, denoised, scaled_dual, measured, lenslet_psf, kernel, layer_bias, mix_weight):
    count = planes.shape[0]
    rim = KS // 2
    kernels = lenslet_psf.astype(jnp.float32)
    planes_half = lax.optimization_barrier(planes.astype(jnp.bfloat16)).astype(jnp.float32)
    numbers = ("NCHW", "OIHW", "NCHW")
    per_plane = lax.conv_general_dilated(planes_half[None], kernels[:, None], (1, 1), [(rim, rim), (rim, rim)],
                                         dimension_numbers=numbers, feature_group_count=count,
                                         precision=lax.Precision.HIGHEST)
    sensor = jnp.sum(per_plane[0], axis=0)
    residual = lax.optimization_barrier((sensor - measured).astype(jnp.bfloat16)).astype(jnp.float32)
    flipped = kernels[:, None, ::-1, ::-1]
    gradient = lax.conv_general_dilated(residual[None, None], flipped, (1, 1), [(rim, rim), (rim, rim)],
                                        dimension_numbers=numbers, precision=lax.Precision.HIGHEST)[0]
    new_planes = planes - step_size * (gradient + penalty * (planes - (denoised - scaled_dual)))
    noisy = new_planes + scaled_dual
    noisy_half = noisy.astype(jnp.bfloat16)
    padded = jnp.pad(noisy_half, 1)
    rows_all = planes.shape[1]
    cols_all = planes.shape[2]
    filters = kernel.astype(jnp.float32)
    mixing = mix_weight.astype(jnp.float32)

    def one_plane(index):
        slab = lax.dynamic_slice_in_dim(padded, index, 3, 0)
        taps = []
        for i in range(3):
            for j in range(3):
                for k in range(3):
                    taps.append(slab[i, j:j + rows_all, k:k + cols_all])
        stacked = jnp.stack(taps).astype(jnp.float32)
        hidden = jnp.einsum("kn,khw->nhw", filters, stacked, precision=lax.Precision.HIGHEST)
        hidden = jnp.maximum(hidden + layer_bias[:, None, None], 0.0)
        hidden = lax.optimization_barrier(hidden.astype(jnp.bfloat16)).astype(jnp.float32)
        return jnp.einsum("n,nhw->hw", mixing, hidden, precision=lax.Precision.HIGHEST)

    noise = lax.map(one_plane, jnp.arange(count, dtype=jnp.int32))
    new_denoised = noisy - noise
    new_dual = scaled_dual + new_planes - new_denoised
    return new_planes, new_denoised, new_dual
```

```python
import functools

import jax
import jax.numpy as jnp
from jax import lax
from jax.experimental import pallas as pl
from jax.experimental.pallas import tpu as pltpu
from jax.sharding import Mesh, PartitionSpec as P

STEP = 4.0
HALF = 0.5
BF = jnp.bfloat16
F32 = jnp.float32
VMEM_LIMIT = 56 * 1024 * 1024


def iota(shape, axis):
    return lax.broadcasted_iota(jnp.int32, shape, axis)


def cross4(x0, x1, x2, x3):
    lane = iota(x0.shape, x0.ndim - 1)
    low = lane < 64
    even = (lane // 32) % 2 == 0
    ax = x0.ndim - 1

    def pair(a, b, mask, shift):
        return (
            jnp.where(mask, a, pltpu.roll(b, shift, ax)),
            jnp.where(mask, pltpu.roll(a, 128 - shift, ax), b),
        )

    y0, y2 = pair(x0, x2, low, 64)
    y1, y3 = pair(x1, x3, low, 64)
    z0, z1 = pair(y0, y1, even, 32)
    z2, z3 = pair(y2, y3, even, 32)
    return z0, z1, z2, z3


def to_blocks(src, base, put):
    for t in range(16):
        for h in range(2):
            x = [src[t, pl.ds(base + 4 * h + m, 8, stride=8), :] for m in range(4)]
            for g, z in enumerate(cross4(*x)):
                put(4 * t + g, h, z)


def from_blocks(get, dst):
    for t in range(16):
        for h in range(2):
            z = cross4(*[get(4 * t + g, h) for g in range(4)])
            for m in range(4):
                dst[t, pl.ds(4 * h + m, 8, stride=8), :] = z[m]


def toeplitz(psf, flip, strips, put):
    s = iota((64, 128), 0) - 1
    b = iota((64, 128), 1)
    pick = jnp.where(s == ((30 - b) if flip else b), 1.0, 0.0).astype(BF)
    turned = lax.dot_general(pick, psf, (((1,), (1,)), ((), ())), preferred_element_type=F32).astype(BF)
    a = iota((32, 1536), 0)
    u = iota((32, 1536), 1) // 32
    spread = jnp.where(a == ((u - 8) if flip else (38 - u)), 1.0, 0.0).astype(BF)
    strip = jnp.dot(turned, spread, preferred_element_type=F32)
    j = iota((64, 1536), 1) % 32
    for bit in (1, 2, 4, 8, 16):
        strip = jnp.where((j & bit) != 0, pltpu.roll(strip, bit, 0), strip)
    for k in range(4):
        moved = strip if k == 0 else pltpu.roll(strip, 1536 - 32 * k, 1)
        strips[k] = moved.astype(BF)
    for d in range(5):
        for i in range(8):
            u0 = 23 - 8 * (d - 2) - i
            cut = slice(128 * (u0 // 4), 128 * (u0 // 4) + 256)
            at = 512 * d + 32 * i
            put(at, strips[u0 % 4, 16:48, cut])
            put(at + 256, strips[u0 % 4, 48:64, cut])
            put(at + 272, strips[u0 % 4, 0:16, cut])


def weights_kernel(psf_ref, kernel_ref, bias_ref, mix_ref, wf_ref, wd_ref, mx_ref, strips, taps, rim):
    def put(at, value):
        wf_ref[at : at + value.shape[0], :] = value

    toeplitz(psf_ref[...], False, strips, put)
    n_of = jnp.where(iota((16, 1024), 1) // 64 == iota((16, 1024), 0), 1.0, 0.0).astype(BF)
    taps[0:27, :] = jnp.dot(kernel_ref[...], n_of, preferred_element_type=F32)
    lane = iota((32, 1024), 1)
    j = lane % 32
    r = (lane // 32) % 2
    jp = iota((32, 1024), 0)
    lane1 = iota((1, 1024), 1)
    j1 = lane1 % 32
    r1 = (lane1 // 32) % 2
    rim[...] = jnp.zeros_like(rim)
    for d in range(3):
        for w in range(4):
            total = jnp.zeros((32, 1024), F32)
            right = jnp.zeros((1, 1024), F32)
            left = jnp.zeros((1, 1024), F32)
            for u in range(3):
                if w - u not in (0, 1):
                    continue
                for v in range(3):
                    row = taps[9 * d + 3 * u + v : 9 * d + 3 * u + v + 1, :]
                    total = jnp.where((r == w - u) & (jp == j + (v - 1)), row, total)
                    if v == 2:
                        right = jnp.where((r1 == w - u) & (j1 == 31), row, right)
                    if v == 0:
                        left = jnp.where((r1 == w - u) & (j1 == 0), row, left)
            wd_ref[(4 * d + w) * 32 : (4 * d + w) * 32 + 32, :] = total.astype(BF)
            at = 32 * w + 2 * d
            rim[at : at + 1, :] = right
            at = (32 * w + 31 + 2 * d) % 128
            rim[at : at + 1, :] = left
    bias = bias_ref[...]
    for at in (6, 7, 8):
        part = bias.astype(BF)
        rim[at : at + 1, :] = jnp.dot(part, n_of, preferred_element_type=F32)
        bias = bias - part.astype(F32)
    wd_ref[384:512, :] = rim[...].astype(BF)
    rows_n = jnp.where(iota((1024, 16), 0) // 64 == iota((1024, 16), 1), 1.0, 0.0).astype(BF)
    mixed = jnp.dot(rows_n, jnp.broadcast_to(mix_ref[...], (16, 128)), preferred_element_type=F32)
    pos = iota((1024, 128), 0) % 64
    lane = iota((1024, 128), 1)
    mx_ref[0:1024, :] = jnp.where(lane == pos, mixed, 0.0).astype(BF)
    mx_ref[1024:2048, :] = jnp.where(lane == pos + 64, mixed, 0.0).astype(BF)


def back_weights_kernel(psf_ref, prev_ref, next_ref, wg_ref, strips):
    for p, ref in enumerate((prev_ref, psf_ref, next_ref)):

        def put(at, value, p=p):
            wg_ref[at : at + value.shape[0], 256 * p : 256 * p + 256] = value

        if p == 1:
            psf = psf_ref[...]
        else:
            psf = jnp.concatenate([ref[g // 2, :, 128 * (g % 2) : 128 * (g % 2) + 128] for g in range(4)], axis=0)
        toeplitz(psf, True, strips, put)


def gather_rows(main, side, lhs):
    j = iota((64, 8, 256), 2) % 32
    for d in range(5):
        lhs[:, 512 * d : 512 * d + 256] = main[1:65, d : d + 8, :].reshape(512, 256).astype(BF)
        rims = jnp.where(j < 16, main[2:66, d : d + 8, :], main[0:64, d : d + 8, :])
        if side is not None:
            side[:, d : d + 8, :] = rims
        lhs[:, 512 * d + 256 : 512 * d + 512] = rims.reshape(512, 256).astype(BF)


def forward_kernel(planes, denoised, dual, measured, lo, hi, psf, wf, part_ref, own_ref, pack_ref,
                   nat, main, lhs, blocks):
    cols = [slice(128 * t, 128 * t + 128) for t in range(16)]
    for t, c in enumerate(cols):
        nat[t, 0:16, :] = lo[0:16, c].astype(F32)
        nat[t, 16:80, :] = planes[:, c].astype(BF).astype(F32)
        nat[t, 80:96, :] = hi[0:16, c].astype(F32)
        nat[t, 96:128, :] = jnp.zeros((32, 128), F32)
    main[0] = jnp.zeros((16, 256), F32)
    main[65] = jnp.zeros((16, 256), F32)
    for half in range(2):

        def put(k, h, z, half=half):
            main[1 + k, 8 * half : 8 * half + 8, 128 * h : 128 * h + 128] = z

        to_blocks(nat, 64 * half, put)
    gather_rows(main, None, lhs)

    def put_measured(k, h, z):
        blocks[8 * k : 8 * k + 8, 128 * h : 128 * h + 128] = z

    for t, c in enumerate(cols):
        nat[t, 0:64, :] = measured[:, c]
    to_blocks(nat, 0, put_measured)
    sums = jnp.dot(lhs[...], wf[...], preferred_element_type=F32)
    part_ref[...] = (sums - blocks[...] * (1.0 / 64)).astype(BF)

    for t, c in enumerate(cols):
        nat[t, 0:8, :] = lo[16:24, c].astype(F32)
        nat[t, 8:72, :] = base(planes[:, c], denoised[:, c], dual[:, c])
        nat[t, 72:80, :] = hi[16:24, c].astype(F32)
    for half in range(2):

        def put(k, h, z, half=half):
            main[k, 8 * half : 8 * half + 8, 128 * h : 128 * h + 128] = z

        to_blocks(nat, 64 * half, put)
    inner = main[0:64, 1:9, :]
    own_ref[...] = inner.reshape(512, 256)
    pack_ref[0:64] = inner.astype(BF)
    lane = iota((64, 128), 1)
    edge = jnp.where(lane >= 96, main[0:64, 0, 128:256], main[0:64, 9, 0:128]).astype(BF)
    for g in range(8):
        pack_ref[64 + g // 2, :, 128 * (g % 2) : 128 * (g % 2) + 128] = edge[8 * g : 8 * g + 8, :]
    for g in range(4):
        pack_ref[68 + g // 2, :, 128 * (g % 2) : 128 * (g % 2) + 128] = psf[8 * g : 8 * g + 8, :]


def base(planes, denoised, dual):
    return planes - STEP * (HALF * (planes - (denoised - dual))) + dual


def final_kernel(valid, planes, denoised, dual, res, res_lo, res_hi, own, own_pack, prev_pack, next_pack, wg, wd, mx,
                 np_ref, nd_ref, du_ref, main, side, lhs, vol, wins, nat, blocks):
    main[0] = jnp.zeros((16, 256), F32)
    main[65] = jnp.zeros((16, 256), F32)
    main[1:65, 0:2, :] = res_lo[...].astype(F32)
    main[1:65, 2:10, :] = res[...].astype(F32).reshape(64, 8, 256)
    main[1:65, 10:12, :] = res_hi[...].astype(F32)
    gather_rows(main, side, lhs)
    grads = jnp.dot(lhs[...], wg[...], preferred_element_type=F32)

    def edge_rows(first):
        parts = []
        for q in range(first, first + 4):
            parts.append(main[1:65, q, :].astype(BF))
            parts.append(side[:, q, :].astype(BF))
        return jnp.concatenate(parts, axis=1)

    above = edge_rows(0)
    below = edge_rows(8)
    lane = iota((64, 128), 1)
    use_lo = valid[0] > 0
    use_hi = valid[1] > 0
    for p, pack in enumerate((prev_pack, own_pack, next_pack)):
        start = own[...] if p == 1 else pack[0:64].astype(F32).reshape(512, 256)
        noisy = start - STEP * grads[:, 256 * p : 256 * p + 256]
        vol[p, 0] = jnp.zeros((16, 256), F32)
        vol[p, 65] = jnp.zeros((16, 256), F32)
        vol[p, 1:65, 1:9, :] = noisy.reshape(64, 8, 256)
        g_lo = jnp.dot(above, wg[512:2560, 256 * p + 128 : 256 * p + 256], preferred_element_type=F32)
        g_hi = jnp.dot(below, wg[0:2048, 256 * p : 256 * p + 128], preferred_element_type=F32)
        edge = jnp.concatenate(
            [pack[64 + g // 2, :, 128 * (g % 2) : 128 * (g % 2) + 128].astype(F32) for g in range(8)], axis=0
        )
        vol[p, 1:65, 0, 128:256] = jnp.where(use_lo, edge - STEP * g_lo, 0.0)
        vol[p, 1:65, 9, 0:128] = jnp.where(use_hi, edge - STEP * g_hi, 0.0)
        for c in range(0, 66, 6):
            t0 = vol[p, c : c + 6, 1:9, 0:128]
            t1 = vol[p, c : c + 6, 1:9, 128:256]
            before = vol[p, c : c + 6, 0:8, 128:256]
            after = vol[p, c : c + 6, 2:10, 0:128]
            group = iota((6, 8, 128), 2) // 32
            up0, up1, upb = (pltpu.roll(x, 32, 2) for x in (t0, t1, before))
            dn0, dn1, dna = (pltpu.roll(x, 96, 2) for x in (t0, t1, after))
            wins[p, 0, c : c + 6] = jnp.where(group == 0, upb, up0)
            wins[p, 2, c : c + 6] = jnp.where(group == 0, up0, up1)
            wins[p, 1, c : c + 6] = jnp.where(group == 3, dn1, dn0)
            wins[p, 3, c : c + 6] = jnp.where(group == 3, dna, dn1)
    lane = iota((8, 8, 128), 2)
    j = lane % 32
    ones = (lane >= 6) & (lane <= 8)
    for k in range(4):
        for c in range(0, 64, 8):
            rim = jnp.zeros((8, 8, 128), F32)
            for p in range(3):
                mid = wins[p, k, c + 1 : c + 9]
                lhs[8 * c : 8 * c + 64, 512 * k + 128 * p : 512 * k + 128 * p + 128] = mid.reshape(64, 128).astype(BF)
                e = jnp.where(j == 0, wins[p, k, c + 2 : c + 10], jnp.where(j == 31, wins[p, k, c : c + 8], 0.0))
                rim = rim + (e if p == 0 else pltpu.roll(e, 2 * p, 2))
            rim = jnp.where(ones, 1.0, rim)
            lhs[8 * c : 8 * c + 64, 512 * k + 384 : 512 * k + 512] = rim.reshape(64, 128).astype(BF)
    for half in range(2):
        total = None
        for e in range(2):
            k = 2 * half + e
            hidden = jnp.dot(lhs[:, 512 * k : 512 * k + 512], wd[...], preferred_element_type=F32)
            hidden = jnp.maximum(hidden, 0.0).astype(BF)
            noise = jnp.dot(hidden, mx[1024 * e : 1024 * e + 1024, :], preferred_element_type=F32)
            total = noise if total is None else total + noise
        blocks[:, 128 * half : 128 * half + 128] = total
    from_blocks(lambda k, h: blocks[8 * k : 8 * k + 8, 128 * h : 128 * h + 128], nat.at[1])
    blocks[...] = grads[:, 256:512]
    from_blocks(lambda k, h: blocks[8 * k : 8 * k + 8, 128 * h : 128 * h + 128], nat.at[0])
    for t in range(16):
        c = slice(128 * t, 128 * t + 128)
        x = planes[:, c]
        z = dual[:, c]
        moved = x - STEP * (nat[0, t] + HALF * (x - (denoised[:, c] - z)))
        cleaned = (moved + z) - nat[1, t]
        np_ref[:, c] = moved
        nd_ref[:, c] = cleaned
        du_ref[:, c] = z + moved - cleaned


def call(body, outs, scratch, n_in, flops=1_000_000_000, smem=0):
    specs = [pl.BlockSpec(memory_space=pltpu.SMEM)] * smem + [pl.BlockSpec(memory_space=pltpu.VMEM)] * (n_in - smem)
    return pl.pallas_call(
        body,
        out_shape=outs,
        in_specs=specs,
        out_specs=[pl.BlockSpec(memory_space=pltpu.VMEM)] * len(outs),
        scratch_shapes=scratch,
        compiler_params=pltpu.CompilerParams(vmem_limit_bytes=VMEM_LIMIT),
        cost_estimate=pl.CostEstimate(flops=flops, bytes_accessed=4_000_000, transcendentals=0),
    )


def out(shape, dtype):
    return jax.ShapeDtypeStruct(shape, dtype)


def all_sum(part):
    group = ("xh", "y", "zl")
    got = lax.all_to_all(part, group, 0, 0, tiled=True)
    mine = jnp.sum(got.reshape(16, 32, 256).astype(F32), axis=0).astype(BF)
    for bit in (2, 1):
        other = lax.ppermute(mine, "zh", [(a, a ^ bit) for a in range(4)])
        mine = (mine.astype(F32) + other.astype(F32)).astype(BF)
    wide = jnp.broadcast_to(mine[None], (16, 32, 256)).reshape(512, 256)
    return lax.all_to_all(wide, group, 0, 0, tiled=True)


def shards(planes, denoised, dual, measured, psf, kernel, bias, mix):
    depth = ("xh", "y", "zh", "zl")
    x, d, z = planes[0], denoised[0], dual[0]
    psf_pad = jnp.pad(psf[0], ((0, 1), (0, 97)))

    def pack(rows, octet):
        edge = base(x[octet], d[octet], z[octet])
        return jnp.concatenate([x[rows].astype(BF), edge.astype(BF)], axis=0)

    down = [(i, i + 1) for i in range(3)]
    up = [(i + 1, i) for i in range(3)]
    lo = lax.ppermute(pack(slice(48, 64), slice(56, 64)), "band", down)
    hi = lax.ppermute(pack(slice(0, 16), slice(0, 8)), "band", up)
    wf, wd, mx = call(
        weights_kernel,
        [out((2560, 256), BF), out((512, 1024), BF), out((2048, 128), BF)],
        [pltpu.VMEM((4, 64, 1536), BF), pltpu.VMEM((32, 1024), F32), pltpu.VMEM((128, 1024), F32)],
        4,
    )(psf_pad, kernel, bias.reshape(1, 16), mix.reshape(16, 1))
    part, own, packed = call(
        forward_kernel,
        [out((512, 256), BF), out((512, 256), F32), out((70, 8, 256), BF)],
        [
            pltpu.VMEM((16, 128, 128), F32),
            pltpu.VMEM((66, 16, 256), F32),
            pltpu.VMEM((512, 2560), BF),
            pltpu.VMEM((512, 256), F32),
        ],
        8,
    )(x, d, z, measured, lo, hi, psf_pad, wf)
    later = [(i, i + 1) for i in range(63)]
    earlier = [(i + 1, i) for i in range(63)]
    prev_pack = lax.ppermute(packed, depth, later)
    next_pack = lax.ppermute(packed, depth, earlier)
    res = all_sum(part)
    res3 = res.reshape(64, 8, 256)
    res_lo = lax.ppermute(res3[:, 6:8], "band", down)
    res_hi = lax.ppermute(res3[:, 0:2], "band", up)
    (wg,) = call(back_weights_kernel, [out((2560, 768), BF)], [pltpu.VMEM((4, 64, 1536), BF)], 3)(
        psf_pad, prev_pack[68:70], next_pack[68:70]
    )
    band = lax.axis_index("band")
    valid = jnp.stack([(band > 0).astype(jnp.int32), (band < 3).astype(jnp.int32)])
    outs = call(
        final_kernel,
        [out((64, 2048), F32)] * 3,
        [
            pltpu.VMEM((66, 16, 256), F32),
            pltpu.VMEM((64, 16, 256), F32),
            pltpu.VMEM((512, 2560), BF),
            pltpu.VMEM((3, 66, 16, 256), F32),
            pltpu.VMEM((3, 4, 66, 8, 128), F32),
            pltpu.VMEM((2, 16, 64, 128), F32),
            pltpu.VMEM((512, 256), F32),
        ],
        14,
        flops=10_000_000_000,
        smem=1,
    )(valid, x, d, z, res, res_lo, res_hi, own, packed, prev_pack, next_pack, wg, wd, mx)
    return tuple(o[None] for o in outs)


def solution(mesh):
    fine = Mesh(mesh.devices.reshape(2, 4, 4, 2, 4), ("xh", "y", "zh", "zl", "band"))
    depth = ("xh", "y", "zh", "zl")
    volume = P(depth, "band", None)
    in_specs = (volume, volume, volume, P("band", None), P(depth, None, None), P(), P(), P())
    return jax.shard_map(shards, mesh=fine, in_specs=in_specs, out_specs=(volume,) * 3, check_vma=False)
```

```python
import jax
import jax.numpy as jnp
from jax import lax
from jax.experimental import pallas as pl
from jax.experimental.pallas import tpu as pltpu
from jax.sharding import Mesh, PartitionSpec as P

STEP = 4.0
HALF = 0.5
BF = jnp.bfloat16
F32 = jnp.float32
MIB = 1024 * 1024


def iota(shape, axis):
    return lax.broadcasted_iota(jnp.int32, shape, axis)


def swap_matrix():
    k = iota((512, 512), 0)
    n = iota((512, 512), 1)
    return jnp.where(n == 128 * ((k // 32) % 4) + 32 * (k // 128) + k % 32, 1.0, 0.0).astype(BF)


def split(x):
    high = x.astype(BF)
    return high, (x - high.astype(F32)).astype(BF)


def toeplitz(psf, flip, strips, put, scale=1.0, turn=0):
    s = iota((64, 128), 0) - 1
    b = iota((64, 128), 1)
    pick = jnp.where(s == ((30 - b) if flip else b), 1.0, 0.0).astype(BF)
    turned = lax.dot_general(pick, psf, (((1,), (1,)), ((), ())), preferred_element_type=F32).astype(BF)
    a = iota((32, 1536), 0)
    u = iota((32, 1536), 1) // 32
    spread = jnp.where(a == ((u - 8) if flip else (38 - u)), scale, 0.0).astype(BF)
    strip = jnp.dot(turned, spread, preferred_element_type=F32)
    j = (iota((64, 1536), 1) - turn + 32) % 32
    for bit in (1, 2, 4, 8, 16):
        strip = jnp.where((j & bit) != 0, pltpu.roll(strip, bit, 0), strip)
    for k in range(4):
        moved = strip if k == 0 else pltpu.roll(strip, 1536 - 32 * k, 1)
        strips[k] = moved.astype(BF)
    for d in range(5):
        for i in range(8):
            u0 = 23 - 8 * (d - 2) - i
            cut = slice(128 * (u0 // 4), 128 * (u0 // 4) + 256)
            at = 512 * d + 32 * i
            put(at, strips[u0 % 4, 16:48, cut])
            put(at + 256, strips[u0 % 4, 48:64, cut])
            put(at + 272, strips[u0 % 4, 0:16, cut])


TURN = (2, 0, 4)


def forward_weights_kernel(psf_ref, wf_ref, strips):
    def put(at, value):
        wf_ref[at : at + value.shape[0], :] = value

    toeplitz(unpack_psf(psf_ref), False, strips, put)


def denoiser_weights_kernel(kernel_ref, bias_ref, mix_ref, even_ref, odd_ref, mx_ref, taps, rims):
    n_of = jnp.where(iota((16, 1024), 1) // 64 == iota((16, 1024), 0), 1.0, 0.0).astype(BF)
    taps[0:27, :] = jnp.dot(kernel_ref[...], n_of, preferred_element_type=F32)
    lane = iota((32, 1024), 1)
    j = lane % 32
    r = (lane // 32) % 2
    lane1 = iota((1, 1024), 1)
    j1 = lane1 % 32
    r1 = (lane1 // 32) % 2
    rims[...] = jnp.zeros_like(rims)
    for d in range(3):
        jp = (iota((32, 1024), 0) - TURN[d] + 32) % 32
        for w in range(4):
            total = jnp.zeros((32, 1024), F32)
            right = jnp.zeros((1, 1024), F32)
            left = jnp.zeros((1, 1024), F32)
            for u in range(3):
                if w - u not in (0, 1):
                    continue
                for v in range(3):
                    row = taps[9 * d + 3 * u + v : 9 * d + 3 * u + v + 1, :]
                    total = jnp.where((r == w - u) & (jp == j + (v - 1)), row, total)
                    if v == 2:
                        right = jnp.where((r1 == w - u) & (j1 == 31), row, right)
                    if v == 0:
                        left = jnp.where((r1 == w - u) & (j1 == 0), row, left)
            for odd, ref in enumerate((even_ref, odd_ref)):
                group = (w + (1 if odd else 3)) % 4
                ref[(4 * d + group) * 32 : (4 * d + group) * 32 + 32, :] = total.astype(BF)
                at = 32 * group + TURN[d]
                rims[odd, at : at + 1, :] = right
                at = 32 * group + (31 + TURN[d]) % 32
                rims[odd, at : at + 1, :] = left
    bias = bias_ref[...]
    for at in (6, 7, 8):
        part = bias.astype(BF)
        row = jnp.dot(part, n_of, preferred_element_type=F32)
        rims[0, at : at + 1, :] = row
        rims[1, at : at + 1, :] = row
        bias = bias - part.astype(F32)
    even_ref[384:512, :] = rims[0].astype(BF)
    odd_ref[384:512, :] = rims[1].astype(BF)
    rows_n = jnp.where(iota((1024, 16), 0) // 64 == iota((1024, 16), 1), 1.0, 0.0).astype(BF)
    mixed = jnp.dot(rows_n, jnp.broadcast_to(mix_ref[...], (16, 128)), preferred_element_type=F32)
    pos = iota((1024, 128), 0) % 64
    lane = iota((1024, 128), 1)
    mx_ref[0:1024, :] = jnp.where(lane == pos, mixed, 0.0).astype(BF)
    mx_ref[1024:2048, :] = jnp.where(lane == pos + 64, mixed, 0.0).astype(BF)


def unpack_psf(ref):
    return jnp.concatenate([ref[64 + g // 2, :, 128 * (g % 2) : 128 * (g % 2) + 128] for g in range(4)], axis=0)


def back_weights_kernel(prev_pack, own_pack, next_pack, wg_ref, down_ref, up_ref, strips, wide):
    down_ref[64:128, 128:256] = jnp.ones((64, 128), BF)
    up_ref[64:128, 128:256] = jnp.ones((64, 128), BF)
    for p, pack in enumerate((prev_pack, own_pack, next_pack)):

        def put(at, value, p=p):
            wg_ref[at : at + value.shape[0], 256 * p : 256 * p + 256] = value

        toeplitz(unpack_psf(pack), True, strips, put, -STEP, TURN[p])
        wide[...] = pack[0:64].astype(F32)
        at = slice(64 * (p // 2), 64 * (p // 2) + 64)
        lanes = slice(128 * (p % 2), 128 * (p % 2) + 128)
        down_ref[at, lanes] = wide[:, 7, 128:256].astype(BF)
        up_ref[at, lanes] = wide[:, 0, 0:128].astype(BF)


def gather_rows(main, lhs):
    j = iota((64, 8, 256), 2) % 32
    for d in range(5):
        lhs[:, 512 * d : 512 * d + 256] = main[1:65, d : d + 8, :].reshape(512, 256).astype(BF)
        rims = jnp.where(j < 16, main[2:66, d : d + 8, :], main[0:64, d : d + 8, :])
        lhs[:, 512 * d + 256 : 512 * d + 512] = rims.reshape(512, 256).astype(BF)


def base(planes, denoised, dual):
    return planes - STEP * (HALF * (planes - (denoised - dual))) + dual


def octets(nat, t, h, at):
    return jnp.concatenate([nat[t, pl.ds(at + 4 * h + m, 8, stride=8), :] for m in range(4)], axis=1)


def start_kernel(planes, denoised, dual, psf_ref, down_ref, up_ref, pack_ref, low_ref, swap_ref, nat, lhs):
    psf = jnp.pad(psf_ref[...].astype(F32), ((0, 1), (0, 97))).astype(BF)
    down_ref[...] = planes[48:64, :].astype(BF)
    up_ref[...] = planes[0:16, :].astype(BF)
    swap = swap_matrix()
    swap_ref[...] = swap
    for t in range(16):
        c = slice(128 * t, 128 * t + 128)
        nat[t] = base(planes[:, c], denoised[:, c], dual[:, c])
    for t in range(16):
        rows = jnp.concatenate([octets(nat, t, 0, 0), octets(nat, t, 1, 0)], axis=0)
        lhs[0, 16 * t : 16 * t + 16, :], lhs[1, 16 * t : 16 * t + 16, :] = split(rows)
    for part, ref in enumerate((pack_ref, low_ref)):
        moved = jnp.dot(lhs[part], swap, preferred_element_type=F32)
        for t in range(16):
            for g in range(4):
                for h in range(2):
                    at = 16 * t + 8 * h
                    ref[4 * t + g, :, 128 * h : 128 * h + 128] = moved[at : at + 8, 128 * g : 128 * g + 128].astype(BF)
    for g in range(4):
        pack_ref[64 + g // 2, :, 128 * (g % 2) : 128 * (g % 2) + 128] = psf[8 * g : 8 * g + 8, :]


def forward_kernel(planes, measured, lo, hi, wf, swap, part_ref, nat, main, lhs, turn):
    for t in range(16):
        c = slice(128 * t, 128 * t + 128)
        nat[0, t, 0:16, :] = lo[:, c].astype(F32)
        nat[0, t, 16:80, :] = planes[:, c].astype(BF).astype(F32)
        nat[0, t, 80:96, :] = hi[:, c].astype(F32)
        nat[0, t, 96:128, :] = jnp.zeros((32, 128), F32)
        nat[1, t, 0:64, :] = measured[:, c]
    for t in range(16):
        for h in range(2):
            rows = jnp.concatenate([octets(nat.at[0], t, h, 0), octets(nat.at[0], t, h, 64)], axis=0)
            turn[32 * t + 16 * h : 32 * t + 16 * h + 16, :] = rows.astype(BF)
        rows = jnp.concatenate([octets(nat.at[1], t, 0, 0), octets(nat.at[1], t, 1, 0)], axis=0)
        turn[512 + 16 * t : 528 + 16 * t, :], turn[768 + 16 * t : 784 + 16 * t, :] = split(rows)
    moved = jnp.dot(turn[...], swap[...], preferred_element_type=F32)
    main[0] = jnp.zeros((16, 256), F32)
    main[65] = jnp.zeros((16, 256), F32)
    for t in range(16):
        for h in range(2):
            for g in range(4):
                at = 32 * t + 16 * h
                main[1 + 4 * t + g, :, 128 * h : 128 * h + 128] = moved[at : at + 16, 128 * g : 128 * g + 128]
    gather_rows(main, lhs)
    sums = jnp.dot(lhs[...], wf[...], preferred_element_type=F32)
    seen = moved[512:768, :] + moved[768:1024, :]
    for t in range(16):
        for g in range(4):
            k = 4 * t + g
            mine = jnp.concatenate(
                [seen[16 * t + 8 * h : 16 * t + 8 * h + 8, 128 * g : 128 * g + 128] for h in range(2)], axis=1
            )
            part_ref[8 * k : 8 * k + 8, :] = (sums[8 * k : 8 * k + 8, :] - mine * (1.0 / 64)).astype(BF)


def rims_kernel(res, edge_down, edge_up, down_ref, up_ref, wide):
    wide[...] = res[...].astype(F32).reshape(64, 8, 256)
    for at, q in enumerate((6, 7)):
        down_ref[64 * at : 64 * at + 64, :] = wide[:, q, :].astype(BF)
    for at, q in enumerate((0, 1)):
        up_ref[64 * at : 64 * at + 64, :] = wide[:, q, :].astype(BF)
    down_ref[128:256, :] = edge_down[...]
    up_ref[128:256, :] = edge_up[...]


def back_kernel(res, wg, moves_ref, main, lhs):
    main[0] = jnp.zeros((16, 256), F32)
    main[65] = jnp.zeros((16, 256), F32)
    main[1:65, 0:2, :] = jnp.zeros((64, 2, 256), F32)
    main[1:65, 2:10, :] = res[...].astype(F32).reshape(64, 8, 256)
    main[1:65, 10:12, :] = jnp.zeros((64, 2, 256), F32)
    gather_rows(main, lhs)
    moves_ref[...] = jnp.dot(lhs[...], wg[...], preferred_element_type=F32)


def final_kernel(planes, denoised, dual, res, moves, lo, hi, own_low, own_pack, prev_pack, next_pack, wg, even, odd, mx,
                 swap, np_ref, nd_ref, du_ref, main, lhs, vol, wins, nat, turn, mine):
    main[0] = jnp.zeros((16, 256), F32)
    main[65] = jnp.zeros((16, 256), F32)
    main[1:65, 2:10, :] = res[...].astype(F32).reshape(64, 8, 256)
    for at in range(2):
        main[1:65, at, :] = lo[64 * at : 64 * at + 64, :].astype(F32)
        main[1:65, 10 + at, :] = hi[64 * at : 64 * at + 64, :].astype(F32)
    j = iota((64, 256), 1) % 32

    def octet(q):
        rim = jnp.where(j < 16, main[2:66, q, :], main[0:64, q, :])
        return [main[1:65, q, :].astype(BF), rim.astype(BF)]

    rows = {q: octet(q) for q in (0, 1, 2, 3, 8, 9, 10, 11)}
    above = jnp.concatenate(rows[0] + rows[1] + rows[2] + rows[3], axis=1)
    below = jnp.concatenate(rows[8] + rows[9] + rows[10] + rows[11], axis=1)
    none = [jnp.zeros((64, 512), BF)]
    first = jnp.concatenate(
        [jnp.concatenate(rows[0] + rows[1], axis=1), jnp.concatenate(rows[1] + none, axis=1)], axis=0
    )
    last = jnp.concatenate(
        [jnp.concatenate(none + rows[10], axis=1), jnp.concatenate(rows[10] + rows[11], axis=1)], axis=0
    )
    first = jnp.dot(first, wg[0:1024, :], preferred_element_type=F32)
    last = jnp.dot(last, wg[1536:2560, :], preferred_element_type=F32)
    use_lo = lo[192:256, 128:256] > 0
    use_hi = hi[192:256, 128:256] > 0
    row = iota((256, 256), 0)
    col = iota((256, 256), 1)
    for p, pack in enumerate((prev_pack, own_pack, next_pack)):
        start = pack[0:64].reshape(512, 256)
        at = slice(128 + 64 * (p // 2), 192 + 64 * (p // 2))
        lanes = slice(128 * (p % 2), 128 * (p % 2) + 128)
        edge_lo = lo[at, lanes]
        edge_hi = hi[at, lanes]
        if p == 1:
            start = start.astype(F32) + own_low[...].astype(F32).reshape(512, 256)
            edge_lo = edge_lo.astype(F32)
            edge_hi = edge_hi.astype(F32)
        else:
            same = (col // 32 == row // 32) & (col % 32 == (row % 32 + TURN[p]) % 32)
            shift = jnp.where(same, 1.0, 0.0).astype(BF)
            start = jnp.dot(start, shift, preferred_element_type=F32)
            edge_lo = jnp.dot(edge_lo, shift[0:128, 0:128], preferred_element_type=F32)
            edge_hi = jnp.dot(edge_hi, shift[0:128, 0:128], preferred_element_type=F32)
        vol[p, 0] = jnp.zeros((16, 256), F32)
        vol[p, 65] = jnp.zeros((16, 256), F32)
        cut = slice(256 * p, 256 * p + 256)
        vol[p, 1:65, 1:9, :] = (start + moves[:, cut]).reshape(64, 8, 256)
        for at in range(2):
            vol[p, 1:65, 1 + at, :] += first[64 * at : 64 * at + 64, cut]
            vol[p, 1:65, 7 + at, :] += last[64 * at : 64 * at + 64, cut]
        if p == 1:
            mine[...] = moves[:, cut].reshape(64, 8, 256)
            for at in range(2):
                mine[:, at, :] += first[64 * at : 64 * at + 64, cut]
                mine[:, 6 + at, :] += last[64 * at : 64 * at + 64, cut]
        g_lo = jnp.dot(above, wg[512:2560, 256 * p + 128 : 256 * p + 256], preferred_element_type=F32)
        g_hi = jnp.dot(below, wg[0:2048, 256 * p : 256 * p + 128], preferred_element_type=F32)
        vol[p, 1:65, 0, 128:256] = jnp.where(use_lo, edge_lo + g_lo, 0.0)
        vol[p, 1:65, 9, 0:128] = jnp.where(use_hi, edge_hi + g_hi, 0.0)
        group = iota((66, 8, 128), 2) // 32
        t0 = vol[p, :, 1:9, 0:128]
        t1 = vol[p, :, 1:9, 128:256]
        wins[p, 0] = jnp.where(group == 3, vol[p, :, 0:8, 128:256], t0)
        wins[p, 1] = jnp.where(group == 0, t1, t0)
        wins[p, 2] = jnp.where(group == 3, t0, t1)
        wins[p, 3] = jnp.where(group == 0, vol[p, :, 2:10, 0:128], t1)
    lane = iota((64, 8, 128), 2)
    j = lane % 32
    ones = jnp.where((lane >= 6) & (lane <= 8), 1.0, 0.0)
    for k in range(4):
        rim = ones
        for p in range(3):
            at = 512 * k + 128 * p
            lhs[:, at : at + 128] = wins[p, k, 1:65].reshape(512, 128).astype(BF)
            rim = jnp.where(j == TURN[p], wins[p, k, 2:66], rim)
            rim = jnp.where(j == (31 + TURN[p]) % 32, wins[p, k, 0:64], rim)
        lhs[:, 512 * k + 384 : 512 * k + 512] = rim.reshape(512, 128).astype(BF)
    noise = []
    for half in range(2):
        total = None
        for e, wd in enumerate((even, odd)):
            k = 2 * half + e
            hidden = jnp.dot(lhs[:, 512 * k : 512 * k + 512], wd[...], preferred_element_type=F32)
            hidden = jnp.maximum(hidden, 0.0).astype(BF)
            part = jnp.dot(hidden, mx[1024 * e : 1024 * e + 1024, :], preferred_element_type=F32)
            total = part if total is None else total + part
        noise.append(total)
    for f in range(2):
        for t in range(16):
            for h in range(2):
                rows = jnp.concatenate(
                    [
                        noise[h][8 * k : 8 * k + 8, :] if f else mine[k, :, 128 * h : 128 * h + 128]
                        for k in range(4 * t, 4 * t + 4)
                    ],
                    axis=1,
                )
                if h == 0:
                    first = rows
            turn[f, 0, 16 * t : 16 * t + 16, :], turn[f, 1, 16 * t : 16 * t + 16, :] = split(
                jnp.concatenate([first, rows], axis=0)
            )
        moved = jnp.dot(turn[f, 0], swap[...], preferred_element_type=F32)
        moved = moved + jnp.dot(turn[f, 1], swap[...], preferred_element_type=F32)
        for t in range(16):
            for h in range(2):
                for m in range(4):
                    at = 16 * t + 8 * h
                    nat[f, t, pl.ds(4 * h + m, 8, stride=8), :] = moved[at : at + 8, 128 * m : 128 * m + 128]
    for t in range(16):
        c = slice(128 * t, 128 * t + 128)
        x = planes[:, c]
        z = dual[:, c]
        moved = (x - STEP * (HALF * (x - (denoised[:, c] - z)))) + nat[0, t]
        cleaned = (moved + z) - nat[1, t]
        np_ref[:, c] = moved
        nd_ref[:, c] = cleaned
        du_ref[:, c] = z + moved - cleaned


def call(body, outs, scratch, n_in, flops=1_000_000_000, vmem=20, specs=None):
    whole = pl.BlockSpec(memory_space=pltpu.VMEM)
    return pl.pallas_call(
        body,
        out_shape=outs,
        in_specs=specs or [whole] * n_in,
        out_specs=[whole] * len(outs),
        scratch_shapes=scratch,
        compiler_params=pltpu.CompilerParams(vmem_limit_bytes=vmem * MIB),
        cost_estimate=pl.CostEstimate(flops=flops, bytes_accessed=4_000_000, transcendentals=0),
    )


def out(shape, dtype):
    return jax.ShapeDtypeStruct(shape, dtype)


def shards(planes, denoised, dual, measured, psf, kernel, bias, mix):
    depth = ("xh", "y", "zh", "zl")
    group = ("xh", "y", "zl")
    x, d, z = planes[0], denoised[0], dual[0]
    down = [(i, i + 1) for i in range(3)]
    up = [(i + 1, i) for i in range(3)]
    later = [(i, i + 1) for i in range(63)]
    earlier = [(i + 1, i) for i in range(63)]

    to_down, to_up, packed, low, swap = call(
        start_kernel,
        [out((16, 2048), BF), out((16, 2048), BF), out((66, 8, 256), BF), out((64, 8, 256), BF), out((512, 512), BF)],
        [pltpu.VMEM((16, 64, 128), F32), pltpu.VMEM((2, 256, 512), BF)],
        4,
    )(x, d, z, psf[0])
    lo = lax.ppermute(to_down, "band", down)
    hi = lax.ppermute(to_up, "band", up)
    prev_pack = lax.ppermute(packed, depth, later)
    next_pack = lax.ppermute(packed, depth, earlier)
    strips = pltpu.VMEM((4, 64, 1536), BF)
    (wf,) = call(forward_weights_kernel, [out((2560, 256), BF)], [strips], 1)(packed)
    (part,) = call(
        forward_kernel,
        [out((512, 256), BF)],
        [
            pltpu.VMEM((2, 16, 128, 128), F32),
            pltpu.VMEM((66, 16, 256), F32),
            pltpu.VMEM((512, 2560), BF),
            pltpu.VMEM((1024, 512), BF),
        ],
        6,
    )(x, measured, lo, hi, wf, swap)
    part, prev_pack, next_pack = lax.optimization_barrier((part, prev_pack, next_pack))
    got = lax.all_to_all(part, group, 0, 0, tiled=True)
    got, prev_pack, own_pack, next_pack, kernel, bias, mix = lax.optimization_barrier(
        (got, prev_pack, packed, next_pack, kernel, bias.reshape(1, 16), mix.reshape(16, 1))
    )
    mine = jnp.sum(got.reshape(16, 32, 256).astype(F32), axis=0)
    other = lax.ppermute(mine, "zh", [(a, a ^ 2) for a in range(4)])
    wg, edge_down, edge_up = call(
        back_weights_kernel,
        [out((2560, 768), BF), out((128, 256), BF), out((128, 256), BF)],
        [strips, pltpu.VMEM((64, 8, 256), F32)],
        3,
    )(prev_pack, own_pack, next_pack)
    mine, wg = lax.optimization_barrier((mine + other, wg))
    other = lax.ppermute(mine, "zh", [(a, a ^ 1) for a in range(4)])
    even, odd, mx = call(
        denoiser_weights_kernel,
        [out((512, 1024), BF), out((512, 1024), BF), out((2048, 128), BF)],
        [pltpu.VMEM((32, 1024), F32), pltpu.VMEM((2, 128, 1024), F32)],
        3,
    )(kernel, bias, mix)
    mine, even = lax.optimization_barrier((mine + other, even))
    wide = jnp.broadcast_to(mine.astype(BF)[None], (16, 32, 256)).reshape(512, 256)
    res = lax.all_to_all(wide, group, 0, 0, tiled=True)
    rim_down, rim_up = call(
        rims_kernel, [out((256, 256), BF), out((256, 256), BF)], [pltpu.VMEM((64, 8, 256), F32)], 3
    )(res, edge_down, edge_up)
    rim_lo = lax.ppermute(rim_down, "band", down)
    rim_hi = lax.ppermute(rim_up, "band", up)
    (moves,) = call(
        back_kernel,
        [out((512, 768), F32)],
        [pltpu.VMEM((66, 16, 256), F32), pltpu.VMEM((512, 2560), BF)],
        2,
    )(res, wg)
    outs = call(
        final_kernel,
        [out((64, 2048), F32)] * 3,
        [
            pltpu.VMEM((66, 16, 256), F32),
            pltpu.VMEM((512, 2048), BF),
            pltpu.VMEM((3, 66, 16, 256), F32),
            pltpu.VMEM((3, 4, 66, 8, 128), F32),
            pltpu.VMEM((2, 16, 64, 128), F32),
            pltpu.VMEM((2, 2, 256, 512), BF),
            pltpu.VMEM((64, 8, 256), F32),
        ],
        16,
        flops=10_000_000_000,
        vmem=36,
    )(x, d, z, res, moves, rim_lo, rim_hi, low, packed, prev_pack, next_pack, wg, even, odd, mx, swap)
    return tuple(o[None] for o in outs)


def solution(mesh):
    fine = Mesh(mesh.devices.reshape(2, 4, 4, 2, 4), ("xh", "y", "zh", "zl", "band"))
    depth = ("xh", "y", "zh", "zl")
    volume = P(depth, "band", None)
    in_specs = (volume, volume, volume, P("band", None), P(depth, None, None), P(), P(), P())
    return jax.shard_map(shards, mesh=fine, in_specs=in_specs, out_specs=(volume,) * 3, check_vma=False)
```

```python
import jax
import jax.numpy as jnp
from jax import lax
from jax.experimental import pallas as pl
from jax.experimental.pallas import tpu as pltpu
from jax.sharding import Mesh, PartitionSpec as P

STEP = 4.0
HALF = 0.5
BF = jnp.bfloat16
F32 = jnp.float32
MIB = 1024 * 1024


def iota(shape, axis):
    return lax.broadcasted_iota(jnp.int32, shape, axis)


def swap_matrix():
    k = iota((512, 512), 0)
    n = iota((512, 512), 1)
    return jnp.where(n == 128 * ((k // 32) % 4) + 32 * (k // 128) + k % 32, 1.0, 0.0).astype(BF)


def split(x):
    high = x.astype(BF)
    return high, (x - high.astype(F32)).astype(BF)


def toeplitz(psf, flip, strips, put, scale=1.0, turn=0):
    s = iota((64, 128), 0) - 1
    b = iota((64, 128), 1)
    pick = jnp.where(s == ((30 - b) if flip else b), 1.0, 0.0).astype(BF)
    turned = lax.dot_general(pick, psf, (((1,), (1,)), ((), ())), preferred_element_type=F32).astype(BF)
    a = iota((32, 1536), 0)
    u = iota((32, 1536), 1) // 32
    spread = jnp.where(a == ((u - 8) if flip else (38 - u)), scale, 0.0).astype(BF)
    strip = jnp.dot(turned, spread, preferred_element_type=F32)
    j = (iota((64, 1536), 1) - turn + 32) % 32
    for bit in (1, 2, 4, 8, 16):
        strip = jnp.where((j & bit) != 0, pltpu.roll(strip, bit, 0), strip)
    for k in range(4):
        moved = strip if k == 0 else pltpu.roll(strip, 1536 - 32 * k, 1)
        strips[k] = moved.astype(BF)
    for d in range(5):
        for i in range(8):
            u0 = 23 - 8 * (d - 2) - i
            cut = slice(128 * (u0 // 4), 128 * (u0 // 4) + 256)
            at = 512 * d + 32 * i
            put(at, strips[u0 % 4, 16:48, cut])
            put(at + 256, strips[u0 % 4, 48:64, cut])
            put(at + 272, strips[u0 % 4, 0:16, cut])


TURN = (2, 0, 4)


def forward_weights_kernel(psf_ref, wf_ref, same_ref, strips):
    def put(at, value):
        wf_ref[at : at + value.shape[0], :] = value

    toeplitz(unpack_psf(psf_ref), False, strips, put)


def denoiser_weights_kernel(kernel_ref, bias_ref, mix_ref, even_ref, odd_ref, mx_ref, taps, rims):
    n_of = jnp.where(iota((16, 1024), 1) // 64 == iota((16, 1024), 0), 1.0, 0.0).astype(BF)
    taps[0:27, :] = jnp.dot(kernel_ref[...], n_of, preferred_element_type=F32)
    lane = iota((32, 1024), 1)
    j = lane % 32
    r = (lane // 32) % 2
    lane1 = iota((1, 1024), 1)
    j1 = lane1 % 32
    r1 = (lane1 // 32) % 2
    rims[...] = jnp.zeros_like(rims)
    for d in range(3):
        jp = (iota((32, 1024), 0) - TURN[d] + 32) % 32
        for w in range(4):
            total = jnp.zeros((32, 1024), F32)
            right = jnp.zeros((1, 1024), F32)
            left = jnp.zeros((1, 1024), F32)
            for u in range(3):
                if w - u not in (0, 1):
                    continue
                for v in range(3):
                    row = taps[9 * d + 3 * u + v : 9 * d + 3 * u + v + 1, :]
                    total = jnp.where((r == w - u) & (jp == j + (v - 1)), row, total)
                    if v == 2:
                        right = jnp.where((r1 == w - u) & (j1 == 31), row, right)
                    if v == 0:
                        left = jnp.where((r1 == w - u) & (j1 == 0), row, left)
            for odd, ref in enumerate((even_ref, odd_ref)):
                group = (w + (1 if odd else 3)) % 4
                ref[(4 * d + group) * 32 : (4 * d + group) * 32 + 32, :] = total.astype(BF)
                at = 32 * group + TURN[d]
                rims[odd, at : at + 1, :] = right
                at = 32 * group + (31 + TURN[d]) % 32
                rims[odd, at : at + 1, :] = left
    bias = bias_ref[...]
    for at in (6, 7, 8):
        part = bias.astype(BF)
        row = jnp.dot(part, n_of, preferred_element_type=F32)
        rims[0, at : at + 1, :] = row
        rims[1, at : at + 1, :] = row
        bias = bias - part.astype(F32)
    even_ref[384:512, :] = rims[0].astype(BF)
    odd_ref[384:512, :] = rims[1].astype(BF)
    rows_n = jnp.where(iota((1024, 16), 0) // 64 == iota((1024, 16), 1), 1.0, 0.0).astype(BF)
    mixed = jnp.dot(rows_n, jnp.broadcast_to(mix_ref[...], (16, 128)), preferred_element_type=F32)
    pos = iota((1024, 128), 0) % 64
    lane = iota((1024, 128), 1)
    mx_ref[0:1024, :] = jnp.where(lane == pos, mixed, 0.0).astype(BF)
    mx_ref[1024:2048, :] = jnp.where(lane == pos + 64, mixed, 0.0).astype(BF)


def unpack_psf(ref):
    return jnp.concatenate([ref[64 + g // 2, :, 128 * (g % 2) : 128 * (g % 2) + 128] for g in range(4)], axis=0)


def back_weights_kernel(prev_pack, own_pack, next_pack, wg_ref, down_ref, up_ref, strips, wide):
    down_ref[64:128, 128:256] = jnp.ones((64, 128), BF)
    up_ref[64:128, 128:256] = jnp.ones((64, 128), BF)
    for p, pack in enumerate((prev_pack, own_pack, next_pack)):

        def put(at, value, p=p):
            wg_ref[at : at + value.shape[0], 256 * p : 256 * p + 256] = value

        toeplitz(unpack_psf(pack), True, strips, put, -STEP, TURN[p])
        wide[...] = pack[0:64].astype(F32)
        at = slice(64 * (p // 2), 64 * (p // 2) + 64)
        lanes = slice(128 * (p % 2), 128 * (p % 2) + 128)
        down_ref[at, lanes] = wide[:, 7, 128:256].astype(BF)
        up_ref[at, lanes] = wide[:, 0, 0:128].astype(BF)


def gather_rows(main, lhs):
    j = iota((64, 8, 256), 2) % 32
    for d in range(5):
        lhs[:, 512 * d : 512 * d + 256] = main[1:65, d : d + 8, :].reshape(512, 256).astype(BF)
        rims = jnp.where(j < 16, main[2:66, d : d + 8, :], main[0:64, d : d + 8, :])
        lhs[:, 512 * d + 256 : 512 * d + 512] = rims.reshape(512, 256).astype(BF)


def base(planes, denoised, dual):
    return planes - STEP * (HALF * (planes - (denoised - dual))) + dual


def octets(nat, t, h, at):
    return jnp.concatenate([nat[t, pl.ds(at + 4 * h + m, 8, stride=8), :] for m in range(4)], axis=1)


def start_kernel(start, psf_ref, pack_ref, low_ref, swap_ref, nat, lhs):
    psf = jnp.pad(psf_ref[...].astype(F32), ((0, 1), (0, 97))).astype(BF)
    swap = swap_matrix()
    swap_ref[...] = swap
    for t in range(16):
        nat[t] = start[:, 128 * t : 128 * t + 128]
    for t in range(16):
        rows = jnp.concatenate([octets(nat, t, 0, 0), octets(nat, t, 1, 0)], axis=0)
        lhs[0, 16 * t : 16 * t + 16, :], lhs[1, 16 * t : 16 * t + 16, :] = split(rows)
    for part, ref in enumerate((pack_ref, low_ref)):
        moved = jnp.dot(lhs[part], swap, preferred_element_type=F32)
        for t in range(16):
            for g in range(4):
                for h in range(2):
                    at = 16 * t + 8 * h
                    ref[4 * t + g, :, 128 * h : 128 * h + 128] = moved[at : at + 8, 128 * g : 128 * g + 128].astype(BF)
    for g in range(4):
        pack_ref[64 + g // 2, :, 128 * (g % 2) : 128 * (g % 2) + 128] = psf[8 * g : 8 * g + 8, :]


def forward_kernel(planes, measured, lo, hi, wf, swap, part_ref, nat, main, lhs, turn):
    for t in range(16):
        c = slice(128 * t, 128 * t + 128)
        nat[0, t, 0:16, :] = lo[:, c].astype(F32)
        nat[0, t, 16:80, :] = planes[:, c].astype(BF).astype(F32)
        nat[0, t, 80:96, :] = hi[:, c].astype(F32)
        nat[0, t, 96:128, :] = jnp.zeros((32, 128), F32)
        nat[1, t, 0:64, :] = measured[:, c]
    for t in range(16):
        for h in range(2):
            rows = jnp.concatenate([octets(nat.at[0], t, h, 0), octets(nat.at[0], t, h, 64)], axis=0)
            turn[32 * t + 16 * h : 32 * t + 16 * h + 16, :] = rows.astype(BF)
        rows = jnp.concatenate([octets(nat.at[1], t, 0, 0), octets(nat.at[1], t, 1, 0)], axis=0)
        turn[512 + 16 * t : 528 + 16 * t, :], turn[768 + 16 * t : 784 + 16 * t, :] = split(rows)
    moved = jnp.dot(turn[...], swap[...], preferred_element_type=F32)
    main[0] = jnp.zeros((16, 256), F32)
    main[65] = jnp.zeros((16, 256), F32)
    for t in range(16):
        for h in range(2):
            for g in range(4):
                at = 32 * t + 16 * h
                main[1 + 4 * t + g, :, 128 * h : 128 * h + 128] = moved[at : at + 16, 128 * g : 128 * g + 128]
    gather_rows(main, lhs)
    sums = jnp.dot(lhs[...], wf[...], preferred_element_type=F32)
    seen = moved[512:768, :] + moved[768:1024, :]
    for t in range(16):
        for g in range(4):
            k = 4 * t + g
            mine = jnp.concatenate(
                [seen[16 * t + 8 * h : 16 * t + 8 * h + 8, 128 * g : 128 * g + 128] for h in range(2)], axis=1
            )
            part_ref[8 * k : 8 * k + 8, :] = (sums[8 * k : 8 * k + 8, :] - mine * (1.0 / 64)).astype(BF)


def rims_kernel(res, edge_down, edge_up, down_ref, up_ref, wide):
    wide[...] = res[...].astype(F32).reshape(64, 8, 256)
    for at, q in enumerate((6, 7)):
        down_ref[64 * at : 64 * at + 64, :] = wide[:, q, :].astype(BF)
    for at, q in enumerate((0, 1)):
        up_ref[64 * at : 64 * at + 64, :] = wide[:, q, :].astype(BF)
    down_ref[128:256, :] = edge_down[...]
    up_ref[128:256, :] = edge_up[...]


def back_kernel(res, wg, moves_ref, main, lhs):
    main[0] = jnp.zeros((16, 256), F32)
    main[65] = jnp.zeros((16, 256), F32)
    main[1:65, 0:2, :] = jnp.zeros((64, 2, 256), F32)
    main[1:65, 2:10, :] = res[...].astype(F32).reshape(64, 8, 256)
    main[1:65, 10:12, :] = jnp.zeros((64, 2, 256), F32)
    gather_rows(main, lhs)
    moves_ref[...] = jnp.dot(lhs[...], wg[...], preferred_element_type=F32)


def final_kernel(planes, denoised, dual, res, moves, lo, hi, own_low, own_pack, prev_pack, next_pack, wg, even, odd, mx,
                 swap, np_ref, nd_ref, du_ref, main, lhs, vol, wins, nat, turn, mine, held, sems):
    main[0] = jnp.zeros((16, 256), F32)
    main[65] = jnp.zeros((16, 256), F32)
    main[1:65, 2:10, :] = res[...].astype(F32).reshape(64, 8, 256)
    for at in range(2):
        main[1:65, at, :] = lo[64 * at : 64 * at + 64, :].astype(F32)
        main[1:65, 10 + at, :] = hi[64 * at : 64 * at + 64, :].astype(F32)
    j = iota((64, 256), 1) % 32

    def octet(q):
        rim = jnp.where(j < 16, main[2:66, q, :], main[0:64, q, :])
        return [main[1:65, q, :].astype(BF), rim.astype(BF)]

    rows = {q: octet(q) for q in (0, 1, 2, 3, 8, 9, 10, 11)}
    above = jnp.concatenate(rows[0] + rows[1] + rows[2] + rows[3], axis=1)
    below = jnp.concatenate(rows[8] + rows[9] + rows[10] + rows[11], axis=1)
    none = [jnp.zeros((64, 512), BF)]
    first = jnp.concatenate(
        [jnp.concatenate(rows[0] + rows[1], axis=1), jnp.concatenate(rows[1] + none, axis=1)], axis=0
    )
    last = jnp.concatenate(
        [jnp.concatenate(none + rows[10], axis=1), jnp.concatenate(rows[10] + rows[11], axis=1)], axis=0
    )
    first = jnp.dot(first, wg[0:1024, :], preferred_element_type=F32)
    last = jnp.dot(last, wg[1536:2560, :], preferred_element_type=F32)
    use_lo = lo[192:256, 128:256] > 0
    use_hi = hi[192:256, 128:256] > 0
    row = iota((256, 256), 0)
    col = iota((256, 256), 1)
    for p, pack in enumerate((prev_pack, own_pack, next_pack)):
        start = pack[0:64].reshape(512, 256)
        at = slice(128 + 64 * (p // 2), 192 + 64 * (p // 2))
        lanes = slice(128 * (p % 2), 128 * (p % 2) + 128)
        edge_lo = lo[at, lanes]
        edge_hi = hi[at, lanes]
        if p == 1:
            start = start.astype(F32) + own_low[...].astype(F32).reshape(512, 256)
            edge_lo = edge_lo.astype(F32)
            edge_hi = edge_hi.astype(F32)
        else:
            same = (col // 32 == row // 32) & (col % 32 == (row % 32 + TURN[p]) % 32)
            shift = jnp.where(same, 1.0, 0.0).astype(BF)
            start = jnp.dot(start, shift, preferred_element_type=F32)
            edge_lo = jnp.dot(edge_lo, shift[0:128, 0:128], preferred_element_type=F32)
            edge_hi = jnp.dot(edge_hi, shift[0:128, 0:128], preferred_element_type=F32)
        vol[p, 0] = jnp.zeros((16, 256), F32)
        vol[p, 65] = jnp.zeros((16, 256), F32)
        cut = slice(256 * p, 256 * p + 256)
        vol[p, 1:65, 1:9, :] = (start + moves[:, cut]).reshape(64, 8, 256)
        for at in range(2):
            vol[p, 1:65, 1 + at, :] += first[64 * at : 64 * at + 64, cut]
            vol[p, 1:65, 7 + at, :] += last[64 * at : 64 * at + 64, cut]
        if p == 1:
            mine[...] = moves[:, cut].reshape(64, 8, 256)
            for at in range(2):
                mine[:, at, :] += first[64 * at : 64 * at + 64, cut]
                mine[:, 6 + at, :] += last[64 * at : 64 * at + 64, cut]
        g_lo = jnp.dot(above, wg[512:2560, 256 * p + 128 : 256 * p + 256], preferred_element_type=F32)
        g_hi = jnp.dot(below, wg[0:2048, 256 * p : 256 * p + 128], preferred_element_type=F32)
        vol[p, 1:65, 0, 128:256] = jnp.where(use_lo, edge_lo + g_lo, 0.0)
        vol[p, 1:65, 9, 0:128] = jnp.where(use_hi, edge_hi + g_hi, 0.0)
        group = iota((66, 8, 128), 2) // 32
        t0 = vol[p, :, 1:9, 0:128]
        t1 = vol[p, :, 1:9, 128:256]
        wins[p, 0] = jnp.where(group == 3, vol[p, :, 0:8, 128:256], t0)
        wins[p, 1] = jnp.where(group == 0, t1, t0)
        wins[p, 2] = jnp.where(group == 3, t0, t1)
        wins[p, 3] = jnp.where(group == 0, vol[p, :, 2:10, 0:128], t1)
    lane = iota((64, 8, 128), 2)
    j = lane % 32
    ones = jnp.where((lane >= 6) & (lane <= 8), 1.0, 0.0)
    for k in range(4):
        rim = ones
        for p in range(3):
            at = 512 * k + 128 * p
            lhs[:, at : at + 128] = wins[p, k, 1:65].reshape(512, 128).astype(BF)
            rim = jnp.where(j == TURN[p], wins[p, k, 2:66], rim)
            rim = jnp.where(j == (31 + TURN[p]) % 32, wins[p, k, 0:64], rim)
        lhs[:, 512 * k + 384 : 512 * k + 512] = rim.reshape(512, 128).astype(BF)
    noise = []
    for half in range(2):
        total = None
        for e, wd in enumerate((even, odd)):
            k = 2 * half + e
            hidden = jnp.dot(lhs[:, 512 * k : 512 * k + 512], wd[...], preferred_element_type=F32)
            hidden = jnp.maximum(hidden, 0.0).astype(BF)
            part = jnp.dot(hidden, mx[1024 * e : 1024 * e + 1024, :], preferred_element_type=F32)
            total = part if total is None else total + part
        noise.append(total)
    for f in range(2):
        for t in range(16):
            for h in range(2):
                rows = jnp.concatenate(
                    [
                        noise[h][8 * k : 8 * k + 8, :] if f else mine[k, :, 128 * h : 128 * h + 128]
                        for k in range(4 * t, 4 * t + 4)
                    ],
                    axis=1,
                )
                if h == 0:
                    first = rows
            turn[f, 0, 16 * t : 16 * t + 16, :], turn[f, 1, 16 * t : 16 * t + 16, :] = split(
                jnp.concatenate([first, rows], axis=0)
            )
        moved = jnp.dot(turn[f, 0], swap[...], preferred_element_type=F32)
        moved = moved + jnp.dot(turn[f, 1], swap[...], preferred_element_type=F32)
        for t in range(16):
            for h in range(2):
                for m in range(4):
                    at = 16 * t + 8 * h
                    nat[f, t, pl.ds(4 * h + m, 8, stride=8), :] = moved[at : at + 8, 128 * m : 128 * m + 128]
    copies = []

    def send(a, ref, c):
        copy = pltpu.make_async_copy(held.at[a, c], ref.at[:, pl.ds(512 * c, 512)], sems.at[a, c])
        copy.start()
        copies.append(copy)

    for c in range(4):
        for t in range(4):
            cut = slice(512 * c + 128 * t, 512 * c + 128 * t + 128)
            at = slice(128 * t, 128 * t + 128)
            x = planes[:, cut]
            z = dual[:, cut]
            moved = (x - STEP * (HALF * (x - (denoised[:, cut] - z)))) + nat[0, 4 * c + t]
            cleaned = (moved + z) - nat[1, 4 * c + t]
            held[0, c, :, at] = moved
            held[1, c, :, at] = cleaned
            held[2, c, :, at] = z + moved - cleaned
        for a, ref in enumerate((np_ref, nd_ref, du_ref)):
            send(a, ref, c)
    for copy in copies:
        copy.wait()


def call(body, outs, scratch, n_in, flops=1_000_000_000, vmem=20, far_out=False, aliases=None):
    whole = pl.BlockSpec(memory_space=pltpu.VMEM)
    distant = pl.BlockSpec(memory_space=pltpu.HBM)
    return pl.pallas_call(
        body,
        out_shape=outs,
        in_specs=[whole] * n_in,
        out_specs=[distant if far_out else whole] * len(outs),
        scratch_shapes=scratch,
        input_output_aliases=aliases or {},
        compiler_params=pltpu.CompilerParams(vmem_limit_bytes=vmem * MIB),
        cost_estimate=pl.CostEstimate(flops=flops, bytes_accessed=4_000_000, transcendentals=0),
    )


def out(shape, dtype):
    return jax.ShapeDtypeStruct(shape, dtype)


def shards(planes, denoised, dual, measured, psf, kernel, bias, mix):
    depth = ("xh", "y", "zh", "zl")
    group = ("xh", "y", "zl")
    x, d, z = planes[0], denoised[0], dual[0]
    down = [(i, i + 1) for i in range(3)]
    up = [(i + 1, i) for i in range(3)]
    later = [(i, i + 1) for i in range(63)]
    earlier = [(i + 1, i) for i in range(63)]

    lo = lax.ppermute(x[48:64].astype(BF), "band", down)
    hi = lax.ppermute(x[0:16].astype(BF), "band", up)
    packed, low, swap = call(
        start_kernel,
        [out((66, 8, 256), BF), out((64, 8, 256), BF), out((512, 512), BF)],
        [pltpu.VMEM((16, 64, 128), F32), pltpu.VMEM((2, 256, 512), BF)],
        2,
        vmem=12,
    )(base(x, d, z), psf[0])
    strips = pltpu.VMEM((4, 64, 1536), BF)
    wf, packed = call(
        forward_weights_kernel,
        [out((2560, 256), BF), out((66, 8, 256), BF)],
        [strips],
        1,
        vmem=8,
        aliases={0: 1},
    )(packed)
    prev_pack = lax.ppermute(packed, depth, later)
    next_pack = lax.ppermute(packed, depth, earlier)
    (part,) = call(
        forward_kernel,
        [out((512, 256), BF)],
        [
            pltpu.VMEM((2, 16, 128, 128), F32),
            pltpu.VMEM((66, 16, 256), F32),
            pltpu.VMEM((512, 2560), BF),
            pltpu.VMEM((1024, 512), BF),
        ],
        6,
    )(x, measured, lo, hi, wf, swap)
    part, prev_pack, next_pack = lax.optimization_barrier((part, prev_pack, next_pack))
    got = lax.all_to_all(part, group, 0, 0, tiled=True)
    mine = jnp.sum(got.reshape(16, 32, 256).astype(F32), axis=0)
    others = [lax.ppermute(mine, "zh", [(a, a ^ bits) for a in range(4)]) for bits in (2, 1, 3)]
    wg, edge_down, edge_up = call(
        back_weights_kernel,
        [out((2560, 768), BF), out((128, 256), BF), out((128, 256), BF)],
        [strips, pltpu.VMEM((64, 8, 256), F32)],
        3,
        vmem=10,
    )(prev_pack, packed, next_pack)
    even, odd, mx = call(
        denoiser_weights_kernel,
        [out((512, 1024), BF), out((512, 1024), BF), out((2048, 128), BF)],
        [pltpu.VMEM((32, 1024), F32), pltpu.VMEM((2, 128, 1024), F32)],
        3,
        vmem=8,
    )(kernel, bias.reshape(1, 16), mix.reshape(16, 1))
    mine = (mine + others[0]) + (others[1] + others[2])
    wide = jnp.broadcast_to(mine.astype(BF)[None], (16, 32, 256)).reshape(512, 256)
    res = lax.all_to_all(wide, group, 0, 0, tiled=True)
    rim_down, rim_up = call(
        rims_kernel, [out((256, 256), BF), out((256, 256), BF)], [pltpu.VMEM((64, 8, 256), F32)], 3, vmem=4
    )(res, edge_down, edge_up)
    rim_lo = lax.ppermute(rim_down, "band", down)
    rim_hi = lax.ppermute(rim_up, "band", up)
    (moves,) = call(
        back_kernel,
        [out((512, 768), F32)],
        [pltpu.VMEM((66, 16, 256), F32), pltpu.VMEM((512, 2560), BF)],
        2,
        vmem=14,
    )(res, wg)
    outs = call(
        final_kernel,
        [out((64, 2048), F32)] * 3,
        [
            pltpu.VMEM((66, 16, 256), F32),
            pltpu.VMEM((512, 2048), BF),
            pltpu.VMEM((3, 66, 16, 256), F32),
            pltpu.VMEM((3, 4, 66, 8, 128), F32),
            pltpu.VMEM((2, 16, 64, 128), F32),
            pltpu.VMEM((2, 2, 256, 512), BF),
            pltpu.VMEM((64, 8, 256), F32),
            pltpu.VMEM((3, 4, 64, 512), F32),
            pltpu.SemaphoreType.DMA((3, 4)),
        ],
        16,
        flops=10_000_000_000,
        vmem=32,
        far_out=True,
    )(x, d, z, res, moves, rim_lo, rim_hi, low, packed, prev_pack, next_pack, wg, even, odd, mx, swap)
    return tuple(o[None] for o in outs)


def solution(mesh):
    fine = Mesh(mesh.devices.reshape(2, 4, 4, 2, 4), ("xh", "y", "zh", "zl", "band"))
    depth = ("xh", "y", "zh", "zl")
    volume = P(depth, "band", None)
    in_specs = (volume, volume, volume, P("band", None), P(depth, None, None), P(), P(), P())
    return jax.shard_map(shards, mesh=fine, in_specs=in_specs, out_specs=(volume,) * 3, check_vma=False)
```

```python
import jax
import jax.numpy as jnp
from jax import lax
from jax.experimental import pallas as pl
from jax.experimental.pallas import tpu as pltpu
from jax.sharding import Mesh, PartitionSpec as P

STEP = 4.0
HALF = 0.5
BF = jnp.bfloat16
F32 = jnp.float32
MIB = 1024 * 1024


def iota(shape, axis):
    return lax.broadcasted_iota(jnp.int32, shape, axis)


def swap_matrix():
    k = iota((512, 512), 0)
    n = iota((512, 512), 1)
    return jnp.where(n == 128 * ((k // 32) % 4) + 32 * (k // 128) + k % 32, 1.0, 0.0).astype(BF)


def split(x):
    high = x.astype(BF)
    return high, (x - high.astype(F32)).astype(BF)


def toeplitz(psf, flip, strips, put, scale=1.0, turn=0):
    s = iota((64, 128), 0) - 1
    b = iota((64, 128), 1)
    pick = jnp.where(s == ((30 - b) if flip else b), 1.0, 0.0).astype(BF)
    turned = lax.dot_general(pick, psf, (((1,), (1,)), ((), ())), preferred_element_type=F32).astype(BF)
    a = iota((32, 1536), 0)
    u = iota((32, 1536), 1) // 32
    spread = jnp.where(a == ((u - 8) if flip else (38 - u)), scale, 0.0).astype(BF)
    strip = jnp.dot(turned, spread, preferred_element_type=F32)
    j = (iota((64, 1536), 1) - turn + 32) % 32
    for bit in (1, 2, 4, 8, 16):
        strip = jnp.where((j & bit) != 0, pltpu.roll(strip, bit, 0), strip)
    for k in range(4):
        moved = strip if k == 0 else pltpu.roll(strip, 1536 - 32 * k, 1)
        strips[k] = moved.astype(BF)
    for d in range(5):
        for i in range(8):
            u0 = 23 - 8 * (d - 2) - i
            cut = slice(128 * (u0 // 4), 128 * (u0 // 4) + 256)
            at = 512 * d + 32 * i
            put(at, strips[u0 % 4, 16:48, cut])
            put(at + 256, strips[u0 % 4, 48:64, cut])
            put(at + 272, strips[u0 % 4, 0:16, cut])


TURN = (2, 0, 4)


def forward_weights_kernel(psf_ref, wf_ref, same_ref, strips):
    def put(at, value):
        wf_ref[at : at + value.shape[0], :] = value

    toeplitz(unpack_psf(psf_ref), False, strips, put)


def denoiser_weights_kernel(kernel_ref, bias_ref, mix_ref, even_ref, odd_ref, mx_ref, taps, rims):
    n_of = jnp.where(iota((16, 1024), 1) // 64 == iota((16, 1024), 0), 1.0, 0.0).astype(BF)
    taps[0:27, :] = jnp.dot(kernel_ref[...], n_of, preferred_element_type=F32)
    lane = iota((32, 1024), 1)
    j = lane % 32
    r = (lane // 32) % 2
    lane1 = iota((1, 1024), 1)
    j1 = lane1 % 32
    r1 = (lane1 // 32) % 2
    rims[...] = jnp.zeros_like(rims)
    for d in range(3):
        jp = (iota((32, 1024), 0) - TURN[d] + 32) % 32
        for w in range(4):
            total = jnp.zeros((32, 1024), F32)
            right = jnp.zeros((1, 1024), F32)
            left = jnp.zeros((1, 1024), F32)
            for u in range(3):
                if w - u not in (0, 1):
                    continue
                for v in range(3):
                    row = taps[9 * d + 3 * u + v : 9 * d + 3 * u + v + 1, :]
                    total = jnp.where((r == w - u) & (jp == j + (v - 1)), row, total)
                    if v == 2:
                        right = jnp.where((r1 == w - u) & (j1 == 31), row, right)
                    if v == 0:
                        left = jnp.where((r1 == w - u) & (j1 == 0), row, left)
            for odd, ref in enumerate((even_ref, odd_ref)):
                group = (w + (1 if odd else 3)) % 4
                ref[(4 * d + group) * 32 : (4 * d + group) * 32 + 32, :] = total.astype(BF)
                at = 32 * group + TURN[d]
                rims[odd, at : at + 1, :] = right
                at = 32 * group + (31 + TURN[d]) % 32
                rims[odd, at : at + 1, :] = left
    bias = bias_ref[...]
    for at in (6, 7, 8):
        part = bias.astype(BF)
        row = jnp.dot(part, n_of, preferred_element_type=F32)
        rims[0, at : at + 1, :] = row
        rims[1, at : at + 1, :] = row
        bias = bias - part.astype(F32)
    even_ref[384:512, :] = rims[0].astype(BF)
    odd_ref[384:512, :] = rims[1].astype(BF)
    rows_n = jnp.where(iota((1024, 16), 0) // 64 == iota((1024, 16), 1), 1.0, 0.0).astype(BF)
    mixed = jnp.dot(rows_n, jnp.broadcast_to(mix_ref[...], (16, 128)), preferred_element_type=F32)
    pos = iota((1024, 128), 0) % 64
    lane = iota((1024, 128), 1)
    mx_ref[0:1024, :] = jnp.where(lane == pos, mixed, 0.0).astype(BF)
    mx_ref[1024:2048, :] = jnp.where(lane == pos + 64, mixed, 0.0).astype(BF)


def unpack_psf(ref):
    return jnp.concatenate([ref[64 + g // 2, :, 128 * (g % 2) : 128 * (g % 2) + 128] for g in range(4)], axis=0)


def back_weights_kernel(prev_pack, own_pack, next_pack, low, wg_ref, starts_ref, down_ref, up_ref, strips, wide):
    down_ref[64:128, 128:256] = jnp.ones((64, 128), BF)
    up_ref[64:128, 128:256] = jnp.ones((64, 128), BF)
    row = iota((256, 256), 0)
    col = iota((256, 256), 1)
    for p, pack in enumerate((prev_pack, own_pack, next_pack)):

        def put(at, value, p=p):
            wg_ref[at : at + value.shape[0], 256 * p : 256 * p + 256] = value

        toeplitz(unpack_psf(pack), True, strips, put, -STEP, TURN[p])
        wide[...] = pack[0:64].astype(F32)
        start = wide[...].reshape(512, 256)
        below = wide[:, 7, 128:256].astype(BF)
        above = wide[:, 0, 0:128].astype(BF)
        if p == 1:
            start = start + low[...].astype(F32).reshape(512, 256)
        else:
            same = (col // 32 == row // 32) & (col % 32 == (row % 32 + TURN[p]) % 32)
            shift = jnp.where(same, 1.0, 0.0).astype(BF)
            start = jnp.dot(start.astype(BF), shift, preferred_element_type=F32)
            below = jnp.dot(below, shift[0:128, 0:128], preferred_element_type=F32).astype(BF)
            above = jnp.dot(above, shift[0:128, 0:128], preferred_element_type=F32).astype(BF)
        starts_ref[:, 256 * p : 256 * p + 256] = start
        at = slice(64 * (p // 2), 64 * (p // 2) + 64)
        lanes = slice(128 * (p % 2), 128 * (p % 2) + 128)
        down_ref[at, lanes] = below
        up_ref[at, lanes] = above


def gather_rows(main, lhs):
    j = iota((64, 8, 256), 2) % 32
    for d in range(5):
        lhs[:, 512 * d : 512 * d + 256] = main[1:65, d : d + 8, :].reshape(512, 256).astype(BF)
        rims = jnp.where(j < 16, main[2:66, d : d + 8, :], main[0:64, d : d + 8, :])
        lhs[:, 512 * d + 256 : 512 * d + 512] = rims.reshape(512, 256).astype(BF)


def base(planes, denoised, dual):
    return planes - STEP * (HALF * (planes - (denoised - dual))) + dual


def octets(nat, t, h, at):
    return jnp.concatenate([nat[t, pl.ds(at + 4 * h + m, 8, stride=8), :] for m in range(4)], axis=1)


def start_kernel(start, psf_ref, pack_ref, low_ref, swap_ref, nat, lhs):
    psf = jnp.pad(psf_ref[...].astype(F32), ((0, 1), (0, 97))).astype(BF)
    swap = swap_matrix()
    swap_ref[...] = swap
    for t in range(16):
        nat[t] = start[:, 128 * t : 128 * t + 128]
    for t in range(16):
        rows = jnp.concatenate([octets(nat, t, 0, 0), octets(nat, t, 1, 0)], axis=0)
        lhs[0, 16 * t : 16 * t + 16, :], lhs[1, 16 * t : 16 * t + 16, :] = split(rows)
    for part, ref in enumerate((pack_ref, low_ref)):
        moved = jnp.dot(lhs[part], swap, preferred_element_type=F32)
        for t in range(16):
            for g in range(4):
                for h in range(2):
                    at = 16 * t + 8 * h
                    ref[4 * t + g, :, 128 * h : 128 * h + 128] = moved[at : at + 8, 128 * g : 128 * g + 128].astype(BF)
    for g in range(4):
        pack_ref[64 + g // 2, :, 128 * (g % 2) : 128 * (g % 2) + 128] = psf[8 * g : 8 * g + 8, :]


def forward_kernel(planes, measured, lo, hi, wf, swap, part_ref, nat, main, lhs, turn):
    for t in range(16):
        c = slice(128 * t, 128 * t + 128)
        nat[0, t, 0:16, :] = lo[:, c].astype(F32)
        nat[0, t, 16:80, :] = planes[:, c].astype(BF).astype(F32)
        nat[0, t, 80:96, :] = hi[:, c].astype(F32)
        nat[0, t, 96:128, :] = jnp.zeros((32, 128), F32)
        nat[1, t, 0:64, :] = measured[:, c]
    for t in range(16):
        for h in range(2):
            rows = jnp.concatenate([octets(nat.at[0], t, h, 0), octets(nat.at[0], t, h, 64)], axis=0)
            turn[32 * t + 16 * h : 32 * t + 16 * h + 16, :] = rows.astype(BF)
        rows = jnp.concatenate([octets(nat.at[1], t, 0, 0), octets(nat.at[1], t, 1, 0)], axis=0)
        turn[512 + 16 * t : 528 + 16 * t, :], turn[768 + 16 * t : 784 + 16 * t, :] = split(rows)
    moved = jnp.dot(turn[...], swap[...], preferred_element_type=F32)
    main[0] = jnp.zeros((16, 256), F32)
    main[65] = jnp.zeros((16, 256), F32)
    for t in range(16):
        for h in range(2):
            for g in range(4):
                at = 32 * t + 16 * h
                main[1 + 4 * t + g, :, 128 * h : 128 * h + 128] = moved[at : at + 16, 128 * g : 128 * g + 128]
    gather_rows(main, lhs)
    sums = jnp.dot(lhs[...], wf[...], preferred_element_type=F32)
    seen = moved[512:768, :] + moved[768:1024, :]
    for t in range(16):
        for g in range(4):
            k = 4 * t + g
            mine = jnp.concatenate(
                [seen[16 * t + 8 * h : 16 * t + 8 * h + 8, 128 * g : 128 * g + 128] for h in range(2)], axis=1
            )
            part_ref[8 * k : 8 * k + 8, :] = (sums[8 * k : 8 * k + 8, :] - mine * (1.0 / 64)).astype(BF)


def rims_kernel(res, edge_down, edge_up, down_ref, up_ref, wide):
    wide[...] = res[...].astype(F32).reshape(64, 8, 256)
    for at, q in enumerate((6, 7)):
        down_ref[64 * at : 64 * at + 64, :] = wide[:, q, :].astype(BF)
    for at, q in enumerate((0, 1)):
        up_ref[64 * at : 64 * at + 64, :] = wide[:, q, :].astype(BF)
    down_ref[128:256, :] = edge_down[...]
    up_ref[128:256, :] = edge_up[...]


def edge_tiles(rows, wg, first, at):
    tiles = [wg[first : first + 1024, 256 * p + at : 256 * p + at + 128] for p in range(3)]
    return jnp.concatenate([jnp.dot(rows, tile, preferred_element_type=F32) for tile in tiles], axis=1)


def back_kernel(res, wg, starts, noisy_ref, moves_ref, edges_ref, main, lhs):
    main[0] = jnp.zeros((16, 256), F32)
    main[65] = jnp.zeros((16, 256), F32)
    main[1:65, 0:2, :] = jnp.zeros((64, 2, 256), F32)
    main[1:65, 2:10, :] = res[...].astype(F32).reshape(64, 8, 256)
    main[1:65, 10:12, :] = jnp.zeros((64, 2, 256), F32)
    gather_rows(main, lhs)
    moves = jnp.dot(lhs[...], wg[...], preferred_element_type=F32)
    noisy_ref[...] = starts[...] + moves
    moves_ref[...] = moves[:, 256:512].reshape(64, 8, 256)
    j = iota((64, 256), 1) % 32

    def octet(q):
        rim = jnp.where(j < 16, main[2:66, q, :], main[0:64, q, :])
        return [main[1:65, q, :].astype(BF), rim.astype(BF)]

    edges_ref[0] = edge_tiles(jnp.concatenate(octet(2) + octet(3), axis=1), wg, 1536, 128)
    edges_ref[1] = edge_tiles(jnp.concatenate(octet(8) + octet(9), axis=1), wg, 0, 0)


def final_kernel(planes, denoised, dual, noisy, moves, edges, lo, hi, wg, even, odd, mx, swap, np_ref, nd_ref, du_ref,
                 halo, lhs, vol, nat, turn, mine, held, sems):
    j = iota((64, 256), 1) % 32
    rows = []
    for n, (ref, at) in enumerate(((lo, 0), (lo, 1), (hi, 0), (hi, 1))):
        halo[n, 0:8] = jnp.zeros((8, 256), F32)
        halo[n, 72:80] = jnp.zeros((8, 256), F32)
        halo[n, 8:72] = ref[64 * at : 64 * at + 64, :].astype(F32)
        rim = jnp.where(j < 16, halo[n, 9:73], halo[n, 7:71])
        rows.append([ref[64 * at : 64 * at + 64, :], rim.astype(BF)])
    none = [jnp.zeros((64, 512), BF)]
    above = jnp.concatenate(rows[0] + rows[1], axis=1)
    below = jnp.concatenate(rows[2] + rows[3], axis=1)
    first = jnp.concatenate([above, jnp.concatenate(rows[1] + none, axis=1)], axis=0)
    last = jnp.concatenate([jnp.concatenate(none + rows[2], axis=1), below], axis=0)
    first = jnp.dot(first, wg[0:1024, :], preferred_element_type=F32)
    last = jnp.dot(last, wg[1536:2560, :], preferred_element_type=F32)
    edge_lo = edges[0] + edge_tiles(above, wg, 512, 128)
    edge_hi = edges[1] + edge_tiles(below, wg, 1024, 0)
    use_lo = lo[192:256, 128:256] > 0
    use_hi = hi[192:256, 128:256] > 0
    for p in range(3):
        cut = slice(256 * p, 256 * p + 256)
        tile = slice(128 * p, 128 * p + 128)
        at = slice(128 + 64 * (p // 2), 192 + 64 * (p // 2))
        lanes = slice(128 * (p % 2), 128 * (p % 2) + 128)
        vol[p, 0] = jnp.zeros((16, 256), F32)
        vol[p, 65] = jnp.zeros((16, 256), F32)
        vol[p, 1:65, 1:9, :] = noisy[:, cut].reshape(64, 8, 256)
        for e in range(2):
            vol[p, 1:65, 1 + e, :] += first[64 * e : 64 * e + 64, cut]
            vol[p, 1:65, 7 + e, :] += last[64 * e : 64 * e + 64, cut]
        vol[p, 1:65, 0, 128:256] = jnp.where(use_lo, lo[at, lanes].astype(F32) + edge_lo[:, tile], 0.0)
        vol[p, 1:65, 9, 0:128] = jnp.where(use_hi, hi[at, lanes].astype(F32) + edge_hi[:, tile], 0.0)
    mine[...] = moves[...]
    for e in range(2):
        mine[:, e, :] += first[64 * e : 64 * e + 64, 256:512]
        mine[:, 6 + e, :] += last[64 * e : 64 * e + 64, 256:512]
    for t in range(2):
        lanes = slice(128 * t, 128 * t + 128)
        j = iota((64, 16, 128), 2) % 32
        rim = jnp.where((j >= 6) & (j <= 8), 1.0, 0.0)
        for p in range(3):
            rim = jnp.where(j == TURN[p], vol[p, 2:66, :, lanes], rim)
            rim = jnp.where(j == (31 + TURN[p]) % 32, vol[p, 0:64, :, lanes], rim)
        vol[3, 1:65, :, lanes] = rim
    group = iota((64, 8, 128), 2) // 32
    for p in range(4):
        t0 = vol[p, 1:65, 1:9, 0:128]
        t1 = vol[p, 1:65, 1:9, 128:256]
        windows = (
            jnp.where(group == 3, vol[p, 1:65, 0:8, 128:256], t0),
            jnp.where(group == 0, t1, t0),
            jnp.where(group == 3, t0, t1),
            jnp.where(group == 0, vol[p, 1:65, 2:10, 0:128], t1),
        )
        for k, window in enumerate(windows):
            at = 512 * k + 128 * p
            lhs[:, at : at + 128] = window.reshape(512, 128).astype(BF)
    noise = []
    for half in range(2):
        total = None
        for e, wd in enumerate((even, odd)):
            k = 2 * half + e
            hidden = jnp.dot(lhs[:, 512 * k : 512 * k + 512], wd[...], preferred_element_type=F32)
            hidden = jnp.maximum(hidden, 0.0).astype(BF)
            part = jnp.dot(hidden, mx[1024 * e : 1024 * e + 1024, :], preferred_element_type=F32)
            total = part if total is None else total + part
        noise.append(total)
    for f in range(2):
        for t in range(16):
            for h in range(2):
                rows = jnp.concatenate(
                    [
                        noise[h][8 * k : 8 * k + 8, :] if f else mine[k, :, 128 * h : 128 * h + 128]
                        for k in range(4 * t, 4 * t + 4)
                    ],
                    axis=1,
                )
                if h == 0:
                    first = rows
            turn[f, 0, 16 * t : 16 * t + 16, :], turn[f, 1, 16 * t : 16 * t + 16, :] = split(
                jnp.concatenate([first, rows], axis=0)
            )
        moved = jnp.dot(turn[f, 0], swap[...], preferred_element_type=F32)
        moved = moved + jnp.dot(turn[f, 1], swap[...], preferred_element_type=F32)
        for t in range(16):
            for h in range(2):
                for m in range(4):
                    at = 16 * t + 8 * h
                    nat[f, t, pl.ds(4 * h + m, 8, stride=8), :] = moved[at : at + 8, 128 * m : 128 * m + 128]
    copies = []

    def send(a, ref, c):
        copy = pltpu.make_async_copy(held.at[a, c], ref.at[:, pl.ds(512 * c, 512)], sems.at[a, c])
        copy.start()
        copies.append(copy)

    for c in range(4):
        for t in range(4):
            cut = slice(512 * c + 128 * t, 512 * c + 128 * t + 128)
            at = slice(128 * t, 128 * t + 128)
            x = planes[:, cut]
            z = dual[:, cut]
            moved = (x - STEP * (HALF * (x - (denoised[:, cut] - z)))) + nat[0, 4 * c + t]
            cleaned = (moved + z) - nat[1, 4 * c + t]
            held[0, c, :, at] = moved
            held[1, c, :, at] = cleaned
            held[2, c, :, at] = z + moved - cleaned
        for a, ref in enumerate((np_ref, nd_ref, du_ref)):
            send(a, ref, c)
    for copy in copies:
        copy.wait()


def call(body, outs, scratch, n_in, flops=1_000_000_000, vmem=20, far_out=False, aliases=None):
    whole = pl.BlockSpec(memory_space=pltpu.VMEM)
    distant = pl.BlockSpec(memory_space=pltpu.HBM)
    return pl.pallas_call(
        body,
        out_shape=outs,
        in_specs=[whole] * n_in,
        out_specs=[distant if far_out else whole] * len(outs),
        scratch_shapes=scratch,
        input_output_aliases=aliases or {},
        compiler_params=pltpu.CompilerParams(vmem_limit_bytes=vmem * MIB),
        cost_estimate=pl.CostEstimate(flops=flops, bytes_accessed=4_000_000, transcendentals=0),
    )


def out(shape, dtype):
    return jax.ShapeDtypeStruct(shape, dtype)


def shards(planes, denoised, dual, measured, psf, kernel, bias, mix):
    depth = ("xh", "y", "zh", "zl")
    group = ("xh", "y", "zl")
    x, d, z = planes[0], denoised[0], dual[0]
    down = [(i, i + 1) for i in range(3)]
    up = [(i + 1, i) for i in range(3)]
    later = [(i, i + 1) for i in range(63)]
    earlier = [(i + 1, i) for i in range(63)]

    lo = lax.ppermute(x[48:64].astype(BF), "band", down)
    hi = lax.ppermute(x[0:16].astype(BF), "band", up)
    packed, low, swap = call(
        start_kernel,
        [out((66, 8, 256), BF), out((64, 8, 256), BF), out((512, 512), BF)],
        [pltpu.VMEM((16, 64, 128), F32), pltpu.VMEM((2, 256, 512), BF)],
        2,
        vmem=12,
    )(base(x, d, z), psf[0])
    strips = pltpu.VMEM((4, 64, 1536), BF)
    wf, packed = call(
        forward_weights_kernel,
        [out((2560, 256), BF), out((66, 8, 256), BF)],
        [strips],
        1,
        vmem=8,
        aliases={0: 1},
    )(packed)
    prev_pack = lax.ppermute(packed, depth, later)
    next_pack = lax.ppermute(packed, depth, earlier)
    (part,) = call(
        forward_kernel,
        [out((512, 256), BF)],
        [
            pltpu.VMEM((2, 16, 128, 128), F32),
            pltpu.VMEM((66, 16, 256), F32),
            pltpu.VMEM((512, 2560), BF),
            pltpu.VMEM((1024, 512), BF),
        ],
        6,
    )(x, measured, lo, hi, wf, swap)
    part, prev_pack, next_pack = lax.optimization_barrier((part, prev_pack, next_pack))
    got = lax.all_to_all(part, group, 0, 0, tiled=True)
    mine = jnp.sum(got.reshape(16, 32, 256).astype(F32), axis=0)
    others = [lax.ppermute(mine, "zh", [(a, a ^ bits) for a in range(4)]) for bits in (2, 1, 3)]
    wg, starts, edge_down, edge_up = call(
        back_weights_kernel,
        [out((2560, 768), BF), out((512, 768), F32), out((128, 256), BF), out((128, 256), BF)],
        [strips, pltpu.VMEM((64, 8, 256), F32)],
        4,
        vmem=12,
    )(prev_pack, packed, next_pack, low)
    even, odd, mx = call(
        denoiser_weights_kernel,
        [out((512, 1024), BF), out((512, 1024), BF), out((2048, 128), BF)],
        [pltpu.VMEM((32, 1024), F32), pltpu.VMEM((2, 128, 1024), F32)],
        3,
        vmem=8,
    )(kernel, bias.reshape(1, 16), mix.reshape(16, 1))
    mine = (mine + others[0]) + (others[1] + others[2])
    wide = jnp.broadcast_to(mine.astype(BF)[None], (16, 32, 256)).reshape(512, 256)
    res = lax.all_to_all(wide, group, 0, 0, tiled=True)
    rim_down, rim_up = call(
        rims_kernel, [out((256, 256), BF), out((256, 256), BF)], [pltpu.VMEM((64, 8, 256), F32)], 3, vmem=4
    )(res, edge_down, edge_up)
    rim_lo = lax.ppermute(rim_down, "band", down)
    rim_hi = lax.ppermute(rim_up, "band", up)
    noisy, moves, edges = call(
        back_kernel,
        [out((512, 768), F32), out((64, 8, 256), F32), out((2, 64, 384), F32)],
        [pltpu.VMEM((66, 16, 256), F32), pltpu.VMEM((512, 2560), BF)],
        3,
        vmem=16,
    )(res, wg, starts)
    outs = call(
        final_kernel,
        [out((64, 2048), F32)] * 3,
        [
            pltpu.VMEM((4, 80, 256), F32),
            pltpu.VMEM((512, 2048), BF),
            pltpu.VMEM((4, 66, 16, 256), F32),
            pltpu.VMEM((2, 16, 64, 128), F32),
            pltpu.VMEM((2, 2, 256, 512), BF),
            pltpu.VMEM((64, 8, 256), F32),
            pltpu.VMEM((3, 4, 64, 512), F32),
            pltpu.SemaphoreType.DMA((3, 4)),
        ],
        13,
        flops=10_000_000_000,
        vmem=28,
        far_out=True,
    )(x, d, z, noisy, moves, edges, rim_lo, rim_hi, wg, even, odd, mx, swap)
    return tuple(o[None] for o in outs)


def solution(mesh):
    fine = Mesh(mesh.devices.reshape(2, 4, 4, 2, 4), ("xh", "y", "zh", "zl", "band"))
    depth = ("xh", "y", "zh", "zl")
    volume = P(depth, "band", None)
    in_specs = (volume, volume, volume, P("band", None), P(depth, None, None), P(), P(), P())
    return jax.shard_map(shards, mesh=fine, in_specs=in_specs, out_specs=(volume,) * 3, check_vma=False)
```

```python
import jax
import jax.numpy as jnp
from jax import lax
from jax.experimental import pallas as pl
from jax.experimental.pallas import tpu as pltpu
from jax.sharding import Mesh, PartitionSpec as P

STEP = 4.0
HALF = 0.5
BF = jnp.bfloat16
F32 = jnp.float32
MIB = 1024 * 1024


def iota(shape, axis):
    return lax.broadcasted_iota(jnp.int32, shape, axis)


def swap_matrix():
    k = iota((512, 512), 0)
    n = iota((512, 512), 1)
    return jnp.where(n == 128 * ((k // 32) % 4) + 32 * (k // 128) + k % 32, 1.0, 0.0).astype(BF)


def split(x):
    high = x.astype(BF)
    return high, (x - high.astype(F32)).astype(BF)


def toeplitz(psf, flip, strips, put, scale=1.0, turn=0):
    s = iota((64, 128), 0) - 1
    b = iota((64, 128), 1)
    pick = jnp.where(s == ((30 - b) if flip else b), 1.0, 0.0).astype(BF)
    turned = lax.dot_general(pick, psf, (((1,), (1,)), ((), ())), preferred_element_type=F32).astype(BF)
    a = iota((32, 1536), 0)
    u = iota((32, 1536), 1) // 32
    spread = jnp.where(a == ((u - 8) if flip else (38 - u)), scale, 0.0).astype(BF)
    strip = jnp.dot(turned, spread, preferred_element_type=F32)
    j = (iota((64, 1536), 1) - turn + 32) % 32
    for bit in (1, 2, 4, 8, 16):
        strip = jnp.where((j & bit) != 0, pltpu.roll(strip, bit, 0), strip)
    for k in range(4):
        moved = strip if k == 0 else pltpu.roll(strip, 1536 - 32 * k, 1)
        strips[k] = moved.astype(BF)
    for d in range(5):
        for i in range(8):
            u0 = 23 - 8 * (d - 2) - i
            cut = slice(128 * (u0 // 4), 128 * (u0 // 4) + 256)
            at = 512 * d + 32 * i
            put(at, strips[u0 % 4, 16:48, cut])
            put(at + 256, strips[u0 % 4, 48:64, cut])
            put(at + 272, strips[u0 % 4, 0:16, cut])


TURN = (2, 0, 4)


def forward_weights_kernel(psf_ref, wf_ref, strips):
    def put(at, value):
        wf_ref[at : at + value.shape[0], :] = value

    toeplitz(unpack_psf(psf_ref), False, strips, put)


def denoiser_weights_kernel(kernel_ref, bias_ref, mix_ref, even_ref, odd_ref, mx_ref, taps, rims):
    n_of = jnp.where(iota((16, 1024), 1) // 64 == iota((16, 1024), 0), 1.0, 0.0).astype(BF)
    taps[0:27, :] = jnp.dot(kernel_ref[...], n_of, preferred_element_type=F32)
    lane = iota((32, 1024), 1)
    j = lane % 32
    r = (lane // 32) % 2
    lane1 = iota((1, 1024), 1)
    j1 = lane1 % 32
    r1 = (lane1 // 32) % 2
    rims[...] = jnp.zeros_like(rims)
    for d in range(3):
        jp = (iota((32, 1024), 0) - TURN[d] + 32) % 32
        for w in range(4):
            total = jnp.zeros((32, 1024), F32)
            right = jnp.zeros((1, 1024), F32)
            left = jnp.zeros((1, 1024), F32)
            for u in range(3):
                if w - u not in (0, 1):
                    continue
                for v in range(3):
                    row = taps[9 * d + 3 * u + v : 9 * d + 3 * u + v + 1, :]
                    total = jnp.where((r == w - u) & (jp == j + (v - 1)), row, total)
                    if v == 2:
                        right = jnp.where((r1 == w - u) & (j1 == 31), row, right)
                    if v == 0:
                        left = jnp.where((r1 == w - u) & (j1 == 0), row, left)
            for odd, ref in enumerate((even_ref, odd_ref)):
                group = (w + (1 if odd else 3)) % 4
                ref[(4 * d + group) * 32 : (4 * d + group) * 32 + 32, :] = total.astype(BF)
                at = 32 * group + TURN[d]
                rims[odd, at : at + 1, :] = right
                at = 32 * group + (31 + TURN[d]) % 32
                rims[odd, at : at + 1, :] = left
    bias = bias_ref[...]
    for at in (6, 7, 8):
        part = bias.astype(BF)
        row = jnp.dot(part, n_of, preferred_element_type=F32)
        rims[0, at : at + 1, :] = row
        rims[1, at : at + 1, :] = row
        bias = bias - part.astype(F32)
    even_ref[384:512, :] = rims[0].astype(BF)
    odd_ref[384:512, :] = rims[1].astype(BF)
    rows_n = jnp.where(iota((1024, 16), 0) // 64 == iota((1024, 16), 1), 1.0, 0.0).astype(BF)
    mixed = jnp.dot(rows_n, jnp.broadcast_to(mix_ref[...], (16, 128)), preferred_element_type=F32)
    pos = iota((1024, 128), 0) % 64
    lane = iota((1024, 128), 1)
    mx_ref[0:1024, :] = jnp.where(lane == pos, mixed, 0.0).astype(BF)
    mx_ref[1024:2048, :] = jnp.where(lane == pos + 64, mixed, 0.0).astype(BF)


def unpack_psf(ref):
    return jnp.concatenate([ref[64 + g // 2, :, 128 * (g % 2) : 128 * (g % 2) + 128] for g in range(4)], axis=0)


def back_weights_kernel(prev_pack, own_pack, next_pack, low, wg_ref, starts_ref, down_ref, up_ref, strips, wide):
    down_ref[64:128, 128:256] = jnp.ones((64, 128), BF)
    up_ref[64:128, 128:256] = jnp.ones((64, 128), BF)
    row = iota((256, 256), 0)
    col = iota((256, 256), 1)
    for p, pack in enumerate((prev_pack, own_pack, next_pack)):

        def put(at, value, p=p):
            wg_ref[at : at + value.shape[0], 256 * p : 256 * p + 256] = value

        toeplitz(unpack_psf(pack), True, strips, put, -STEP, TURN[p])
        wide[...] = pack[0:64].astype(F32)
        start = wide[...].reshape(512, 256)
        below = wide[:, 7, 128:256].astype(BF)
        above = wide[:, 0, 0:128].astype(BF)
        if p == 1:
            start = start + low[...].astype(F32).reshape(512, 256)
        else:
            same = (col // 32 == row // 32) & (col % 32 == (row % 32 + TURN[p]) % 32)
            shift = jnp.where(same, 1.0, 0.0).astype(BF)
            start = jnp.dot(start.astype(BF), shift, preferred_element_type=F32)
            below = jnp.dot(below, shift[0:128, 0:128], preferred_element_type=F32).astype(BF)
            above = jnp.dot(above, shift[0:128, 0:128], preferred_element_type=F32).astype(BF)
        starts_ref[:, 256 * p : 256 * p + 256] = start
        at = slice(64 * (p // 2), 64 * (p // 2) + 64)
        lanes = slice(128 * (p % 2), 128 * (p % 2) + 128)
        down_ref[at, lanes] = below
        up_ref[at, lanes] = above


def gather_rows(main, lhs):
    j = iota((64, 8, 256), 2) % 32
    for d in range(5):
        lhs[:, 512 * d : 512 * d + 256] = main[1:65, d : d + 8, :].reshape(512, 256).astype(BF)
        rims = jnp.where(j < 16, main[2:66, d : d + 8, :], main[0:64, d : d + 8, :])
        lhs[:, 512 * d + 256 : 512 * d + 512] = rims.reshape(512, 256).astype(BF)


def base(planes, denoised, dual):
    return planes - STEP * (HALF * (planes - (denoised - dual))) + dual


def octets(nat, t, h, at):
    return jnp.concatenate([nat[t, pl.ds(at + 4 * h + m, 8, stride=8), :] for m in range(4)], axis=1)


def start_kernel(start, psf_ref, pack_ref, low_ref, swap_ref, nat, lhs):
    psf = jnp.pad(psf_ref[...].astype(F32), ((0, 1), (0, 97))).astype(BF)
    swap = swap_matrix()
    swap_ref[...] = swap
    for t in range(16):
        nat[t] = start[:, 128 * t : 128 * t + 128]
    for t in range(16):
        rows = jnp.concatenate([octets(nat, t, 0, 0), octets(nat, t, 1, 0)], axis=0)
        lhs[0, 16 * t : 16 * t + 16, :], lhs[1, 16 * t : 16 * t + 16, :] = split(rows)
    for part, ref in enumerate((pack_ref, low_ref)):
        moved = jnp.dot(lhs[part], swap, preferred_element_type=F32)
        for t in range(16):
            for g in range(4):
                for h in range(2):
                    at = 16 * t + 8 * h
                    ref[4 * t + g, :, 128 * h : 128 * h + 128] = moved[at : at + 8, 128 * g : 128 * g + 128].astype(BF)
    for g in range(4):
        pack_ref[64 + g // 2, :, 128 * (g % 2) : 128 * (g % 2) + 128] = psf[8 * g : 8 * g + 8, :]


def forward_kernel(planes, measured, lo, hi, wf, swap, part_ref, nat, main, lhs, turn):
    for t in range(16):
        c = slice(128 * t, 128 * t + 128)
        nat[0, t, 0:16, :] = lo[:, c].astype(F32)
        nat[0, t, 16:80, :] = planes[:, c].astype(BF).astype(F32)
        nat[0, t, 80:96, :] = hi[:, c].astype(F32)
        nat[0, t, 96:128, :] = jnp.zeros((32, 128), F32)
        nat[1, t, 0:64, :] = measured[:, c]
    for t in range(16):
        for h in range(2):
            rows = jnp.concatenate([octets(nat.at[0], t, h, 0), octets(nat.at[0], t, h, 64)], axis=0)
            turn[32 * t + 16 * h : 32 * t + 16 * h + 16, :] = rows.astype(BF)
        rows = jnp.concatenate([octets(nat.at[1], t, 0, 0), octets(nat.at[1], t, 1, 0)], axis=0)
        turn[512 + 16 * t : 528 + 16 * t, :], turn[768 + 16 * t : 784 + 16 * t, :] = split(rows)
    moved = jnp.dot(turn[...], swap[...], preferred_element_type=F32)
    main[0] = jnp.zeros((16, 256), F32)
    main[65] = jnp.zeros((16, 256), F32)
    for t in range(16):
        for h in range(2):
            for g in range(4):
                at = 32 * t + 16 * h
                main[1 + 4 * t + g, :, 128 * h : 128 * h + 128] = moved[at : at + 16, 128 * g : 128 * g + 128]
    gather_rows(main, lhs)
    sums = jnp.dot(lhs[...], wf[...], preferred_element_type=F32)
    seen = moved[512:768, :] + moved[768:1024, :]
    for t in range(16):
        for g in range(4):
            k = 4 * t + g
            mine = jnp.concatenate(
                [seen[16 * t + 8 * h : 16 * t + 8 * h + 8, 128 * g : 128 * g + 128] for h in range(2)], axis=1
            )
            part_ref[8 * k : 8 * k + 8, :] = (sums[8 * k : 8 * k + 8, :] - mine * (1.0 / 64)).astype(BF)


def rims_kernel(res, edge_down, edge_up, down_ref, up_ref, wide):
    wide[...] = res[...].astype(F32).reshape(64, 8, 256)
    for at, q in enumerate((6, 7)):
        down_ref[64 * at : 64 * at + 64, :] = wide[:, q, :].astype(BF)
    for at, q in enumerate((0, 1)):
        up_ref[64 * at : 64 * at + 64, :] = wide[:, q, :].astype(BF)
    down_ref[128:256, :] = edge_down[...]
    up_ref[128:256, :] = edge_up[...]


def edge_tiles(rows, wg, first, at):
    tiles = [wg[first : first + 1024, 256 * p + at : 256 * p + at + 128] for p in range(3)]
    return jnp.concatenate([jnp.dot(rows, tile, preferred_element_type=F32) for tile in tiles], axis=1)


def back_kernel(res, wg, starts, noisy_ref, moves_ref, edges_ref, main, lhs):
    main[0] = jnp.zeros((16, 256), F32)
    main[65] = jnp.zeros((16, 256), F32)
    main[1:65, 0:2, :] = jnp.zeros((64, 2, 256), F32)
    main[1:65, 2:10, :] = res[...].astype(F32).reshape(64, 8, 256)
    main[1:65, 10:12, :] = jnp.zeros((64, 2, 256), F32)
    gather_rows(main, lhs)
    moves = jnp.dot(lhs[...], wg[...], preferred_element_type=F32)
    noisy_ref[...] = starts[...] + moves
    moves_ref[...] = moves[:, 256:512].reshape(64, 8, 256)
    j = iota((64, 256), 1) % 32

    def octet(q):
        rim = jnp.where(j < 16, main[2:66, q, :], main[0:64, q, :])
        return [main[1:65, q, :].astype(BF), rim.astype(BF)]

    edges_ref[0] = edge_tiles(jnp.concatenate(octet(2) + octet(3), axis=1), wg, 1536, 128)
    edges_ref[1] = edge_tiles(jnp.concatenate(octet(8) + octet(9), axis=1), wg, 0, 0)


def final_kernel(planes, denoised, dual, noisy, moves, edges, lo, hi, wg, even, odd, mx, swap, np_ref, nd_ref, du_ref,
                 halo, lhs, vol, nat, turn, mine, held, sems):
    j = iota((64, 256), 1) % 32
    rows = []
    for n, (ref, at) in enumerate(((lo, 0), (lo, 1), (hi, 0), (hi, 1))):
        halo[n, 0:8] = jnp.zeros((8, 256), F32)
        halo[n, 72:80] = jnp.zeros((8, 256), F32)
        halo[n, 8:72] = ref[64 * at : 64 * at + 64, :].astype(F32)
        rim = jnp.where(j < 16, halo[n, 9:73], halo[n, 7:71])
        rows.append([ref[64 * at : 64 * at + 64, :], rim.astype(BF)])
    none = [jnp.zeros((64, 512), BF)]
    above = jnp.concatenate(rows[0] + rows[1], axis=1)
    below = jnp.concatenate(rows[2] + rows[3], axis=1)
    first = jnp.concatenate([above, jnp.concatenate(rows[1] + none, axis=1)], axis=0)
    last = jnp.concatenate([jnp.concatenate(none + rows[2], axis=1), below], axis=0)
    first = jnp.dot(first, wg[0:1024, :], preferred_element_type=F32)
    last = jnp.dot(last, wg[1536:2560, :], preferred_element_type=F32)
    edge_lo = edges[0] + edge_tiles(above, wg, 512, 128)
    edge_hi = edges[1] + edge_tiles(below, wg, 1024, 0)
    use_lo = lo[192:256, 128:256] > 0
    use_hi = hi[192:256, 128:256] > 0
    for p in range(3):
        cut = slice(256 * p, 256 * p + 256)
        tile = slice(128 * p, 128 * p + 128)
        at = slice(128 + 64 * (p // 2), 192 + 64 * (p // 2))
        lanes = slice(128 * (p % 2), 128 * (p % 2) + 128)
        vol[p, 0] = jnp.zeros((16, 256), F32)
        vol[p, 65] = jnp.zeros((16, 256), F32)
        vol[p, 1:65, 1:9, :] = noisy[:, cut].reshape(64, 8, 256)
        for e in range(2):
            vol[p, 1:65, 1 + e, :] += first[64 * e : 64 * e + 64, cut]
            vol[p, 1:65, 7 + e, :] += last[64 * e : 64 * e + 64, cut]
        vol[p, 1:65, 0, 128:256] = jnp.where(use_lo, lo[at, lanes].astype(F32) + edge_lo[:, tile], 0.0)
        vol[p, 1:65, 9, 0:128] = jnp.where(use_hi, hi[at, lanes].astype(F32) + edge_hi[:, tile], 0.0)
    mine[...] = moves[...]
    for e in range(2):
        mine[:, e, :] += first[64 * e : 64 * e + 64, 256:512]
        mine[:, 6 + e, :] += last[64 * e : 64 * e + 64, 256:512]
    for t in range(2):
        lanes = slice(128 * t, 128 * t + 128)
        j = iota((64, 16, 128), 2) % 32
        rim = jnp.where((j >= 6) & (j <= 8), 1.0, 0.0)
        for p in range(3):
            rim = jnp.where(j == TURN[p], vol[p, 2:66, :, lanes], rim)
            rim = jnp.where(j == (31 + TURN[p]) % 32, vol[p, 0:64, :, lanes], rim)
        vol[3, 1:65, :, lanes] = rim
    group = iota((64, 8, 128), 2) // 32
    for p in range(4):
        t0 = vol[p, 1:65, 1:9, 0:128]
        t1 = vol[p, 1:65, 1:9, 128:256]
        windows = (
            jnp.where(group == 3, vol[p, 1:65, 0:8, 128:256], t0),
            jnp.where(group == 0, t1, t0),
            jnp.where(group == 3, t0, t1),
            jnp.where(group == 0, vol[p, 1:65, 2:10, 0:128], t1),
        )
        for k, window in enumerate(windows):
            at = 512 * k + 128 * p
            lhs[:, at : at + 128] = window.reshape(512, 128).astype(BF)
    noise = []
    for half in range(2):
        total = None
        for e, wd in enumerate((even, odd)):
            k = 2 * half + e
            hidden = jnp.dot(lhs[:, 512 * k : 512 * k + 512], wd[...], preferred_element_type=F32)
            hidden = jnp.maximum(hidden, 0.0).astype(BF)
            part = jnp.dot(hidden, mx[1024 * e : 1024 * e + 1024, :], preferred_element_type=F32)
            total = part if total is None else total + part
        noise.append(total)
    for f in range(2):
        for t in range(16):
            for h in range(2):
                rows = jnp.concatenate(
                    [
                        noise[h][8 * k : 8 * k + 8, :] if f else mine[k, :, 128 * h : 128 * h + 128]
                        for k in range(4 * t, 4 * t + 4)
                    ],
                    axis=1,
                )
                if h == 0:
                    first = rows
            turn[f, 0, 16 * t : 16 * t + 16, :], turn[f, 1, 16 * t : 16 * t + 16, :] = split(
                jnp.concatenate([first, rows], axis=0)
            )
        moved = jnp.dot(turn[f, 0], swap[...], preferred_element_type=F32)
        moved = moved + jnp.dot(turn[f, 1], swap[...], preferred_element_type=F32)
        for t in range(16):
            for h in range(2):
                for m in range(4):
                    at = 16 * t + 8 * h
                    nat[f, t, pl.ds(4 * h + m, 8, stride=8), :] = moved[at : at + 8, 128 * m : 128 * m + 128]
    copies = []

    def send(a, ref, c):
        copy = pltpu.make_async_copy(held.at[a, c], ref.at[:, pl.ds(512 * c, 512)], sems.at[a, c])
        copy.start()
        copies.append(copy)

    for c in range(4):
        for t in range(4):
            cut = slice(512 * c + 128 * t, 512 * c + 128 * t + 128)
            at = slice(128 * t, 128 * t + 128)
            x = planes[:, cut]
            z = dual[:, cut]
            moved = (x - STEP * (HALF * (x - (denoised[:, cut] - z)))) + nat[0, 4 * c + t]
            cleaned = (moved + z) - nat[1, 4 * c + t]
            held[0, c, :, at] = moved
            held[1, c, :, at] = cleaned
            held[2, c, :, at] = z + moved - cleaned
        for a, ref in enumerate((np_ref, nd_ref, du_ref)):
            send(a, ref, c)
    for copy in copies:
        copy.wait()


def call(body, outs, scratch, n_in, flops=1_000_000_000, vmem=20, far_out=False):
    whole = pl.BlockSpec(memory_space=pltpu.VMEM)
    distant = pl.BlockSpec(memory_space=pltpu.HBM)
    return pl.pallas_call(
        body,
        out_shape=outs,
        in_specs=[whole] * n_in,
        out_specs=[distant if far_out else whole] * len(outs),
        scratch_shapes=scratch,
        compiler_params=pltpu.CompilerParams(vmem_limit_bytes=vmem * MIB),
        cost_estimate=pl.CostEstimate(flops=flops, bytes_accessed=4_000_000, transcendentals=0),
    )


def out(shape, dtype):
    return jax.ShapeDtypeStruct(shape, dtype)


def shards(planes, denoised, dual, measured, psf, kernel, bias, mix):
    depth = ("xh", "y", "zh", "zl")
    group = ("xh", "y", "zl")
    x, d, z = planes[0], denoised[0], dual[0]
    down = [(i, i + 1) for i in range(3)]
    up = [(i + 1, i) for i in range(3)]
    later = [(i, i + 1) for i in range(63)]
    earlier = [(i + 1, i) for i in range(63)]

    lo = lax.ppermute(x[48:64].astype(BF), "band", down)
    hi = lax.ppermute(x[0:16].astype(BF), "band", up)
    packed, low, swap = call(
        start_kernel,
        [out((66, 8, 256), BF), out((64, 8, 256), BF), out((512, 512), BF)],
        [pltpu.VMEM((16, 64, 128), F32), pltpu.VMEM((2, 256, 512), BF)],
        2,
        vmem=12,
    )(base(x, d, z), psf[0])
    strips = pltpu.VMEM((4, 64, 1536), BF)
    (wf,) = call(forward_weights_kernel, [out((2560, 256), BF)], [strips], 1, vmem=8)(packed)
    prev_pack = lax.ppermute(packed, depth, later)
    next_pack = lax.ppermute(packed, depth, earlier)
    (part,) = call(
        forward_kernel,
        [out((512, 256), BF)],
        [
            pltpu.VMEM((2, 16, 128, 128), F32),
            pltpu.VMEM((66, 16, 256), F32),
            pltpu.VMEM((512, 2560), BF),
            pltpu.VMEM((1024, 512), BF),
        ],
        6,
    )(x, measured, lo, hi, wf, swap)
    part, prev_pack, next_pack = lax.optimization_barrier((part, prev_pack, next_pack))
    got = lax.all_to_all(part, group, 0, 0, tiled=True)
    mine = jnp.sum(got.reshape(16, 32, 256).astype(F32), axis=0)
    others = [lax.ppermute(mine, "zh", [(a, a ^ bits) for a in range(4)]) for bits in (2, 1, 3)]
    wg, starts, edge_down, edge_up = call(
        back_weights_kernel,
        [out((2560, 768), BF), out((512, 768), F32), out((128, 256), BF), out((128, 256), BF)],
        [strips, pltpu.VMEM((64, 8, 256), F32)],
        4,
        vmem=12,
    )(prev_pack, packed, next_pack, low)
    even, odd, mx = call(
        denoiser_weights_kernel,
        [out((512, 1024), BF), out((512, 1024), BF), out((2048, 128), BF)],
        [pltpu.VMEM((32, 1024), F32), pltpu.VMEM((2, 128, 1024), F32)],
        3,
        vmem=8,
    )(kernel, bias.reshape(1, 16), mix.reshape(16, 1))
    mine = (mine + others[0]) + (others[1] + others[2])
    wide = jnp.broadcast_to(mine.astype(BF)[None], (16, 32, 256)).reshape(512, 256)
    res = lax.all_to_all(wide, group, 0, 0, tiled=True)
    rim_down, rim_up = call(
        rims_kernel, [out((256, 256), BF), out((256, 256), BF)], [pltpu.VMEM((64, 8, 256), F32)], 3, vmem=4
    )(res, edge_down, edge_up)
    rim_lo = lax.ppermute(rim_down, "band", down)
    rim_hi = lax.ppermute(rim_up, "band", up)
    noisy, moves, edges = call(
        back_kernel,
        [out((512, 768), F32), out((64, 8, 256), F32), out((2, 64, 384), F32)],
        [pltpu.VMEM((66, 16, 256), F32), pltpu.VMEM((512, 2560), BF)],
        3,
        vmem=16,
    )(res, wg, starts)
    outs = call(
        final_kernel,
        [out((64, 2048), F32)] * 3,
        [
            pltpu.VMEM((4, 80, 256), F32),
            pltpu.VMEM((512, 2048), BF),
            pltpu.VMEM((4, 66, 16, 256), F32),
            pltpu.VMEM((2, 16, 64, 128), F32),
            pltpu.VMEM((2, 2, 256, 512), BF),
            pltpu.VMEM((64, 8, 256), F32),
            pltpu.VMEM((3, 4, 64, 512), F32),
            pltpu.SemaphoreType.DMA((3, 4)),
        ],
        13,
        flops=10_000_000_000,
        vmem=28,
        far_out=True,
    )(x, d, z, noisy, moves, edges, rim_lo, rim_hi, wg, even, odd, mx, swap)
    return tuple(o[None] for o in outs)


def solution(mesh):
    fine = Mesh(mesh.devices.reshape(2, 4, 4, 2, 4), ("xh", "y", "zh", "zl", "band"))
    depth = ("xh", "y", "zh", "zl")
    volume = P(depth, "band", None)
    in_specs = (volume, volume, volume, P("band", None), P(depth, None, None), P(), P(), P())
    return jax.shard_map(shards, mesh=fine, in_specs=in_specs, out_specs=(volume,) * 3, check_vma=False)
```
